256 devices in a mesh: rep: 8 (over z), region: 32 (over y, x, core).
Axes of the slice: x: 4, y: 4, z: 8, core: 2. Of those that a mesh axis runs over, the one named last changes fastest.
Arguments:
- anchor: float32 [3, 32768], P(None, ('rep', 'region')), may hold values from -4 to 4
- direction: float32 [3, 32768], P(None, ('rep', 'region')), may hold values from -4 to 4
- seg_start: float32 [4, 32768], P(None, ('rep', 'region')), may hold values from 0 to 4
- seg_step: bfloat16 [4, 32768], P(None, ('rep', 'region')), may hold values from 0.019897461 to 0.119628906
- counts: int32 [4, 32768], P(None, ('rep', 'region')), may hold values from 1 to 16
- routes: int32 [32768, 4], P(('rep', 'region')), may hold values from 0 to 127, all different within a row; in each aligned block of 128 rows (0 to 127, 128 to 255, ...) at most 8 rows name the same one
- order: int32 [32768, 4], P(('rep', 'region')), may hold values from 0 to 3, each once within a row
- target: float32 [3, 32768], P(None, ('rep', 'region')), may hold values from 0 to 1
- fourier: float32 [3, 64], replicated, may hold values from -4 to 4
- w_input: bfloat16 [128, 128, 256], P('region'), may hold values from -0.5 to 0.5
- b_input: float32 [128, 256], P('region'), may hold values from -3 to 3
- w_middle: bfloat16 [128, 256, 256], P('region'), may hold values from -0.375 to 0.375
- b_middle: float32 [128, 256], P('region'), may hold values from -3 to 3
- w_output: bfloat16 [128, 4, 256], P('region'), may hold values from -0.375 to 0.375
Outputs:
- rendered: float32 [3, 32768], P(None, ('rep', 'region'))
- grad_w_input: float32 [128, 128, 256], P('region')
- grad_b_input: float32 [128, 256], P('region')
- grad_w_middle: float32 [128, 256, 256], P('region')
- grad_b_middle: float32 [128, 256], P('region')
- grad_w_output: float32 [128, 4, 256], P('region')
The draws below stay inside these ranges and needn't reach their ends.
Inputs may be any that keep to these rules, and one draw needn't show every extreme that they name: `routes`: each ray names 4 different regions; among the rays of one device no region is named more than 8 times, and in every draw some region is named exactly 8 times by the rays of some device. `order`: each row is an ordering of 0 to 3.
All inputs are finite; a program needn't handle non-finite values.
Results may differ from the reference program's by a relative error of at most 0.004.
Values may be sent and summed in bfloat16 or wider, within the bound.
No kernel may reach another device: no remote copies, remote signals or barrier semaphores. Data moves between devices by JAX's collectives and lax.ppermute only.
A program may use at most 192 MiB of HBM per device.

```python
import math
import jax
import jax.numpy as jnp
import numpy as np
from jax import lax

H = 256
ENC = 128
FOURIER = 64
SEG = 16
CROSS = 4
RAYS_DEV = 128
REGIONS = 128
RAYS = 32768
MOST = 8
LOSS_DIV = 16
N_REP = 8
N_REGION = 32


def plant(result, stream_key, smallest, top_value):
    longest = result.shape.index(max(result.shape))
    spots = []
    for shift in (0, 1):
        where = [jax.random.randint(jax.random.fold_in(stream_key, axis), (), 0, length) for axis, length in enumerate(result.shape)]
        where[longest] = (where[longest] + shift) % result.shape[longest]
        spots.append(tuple(where))
    return result.at[spots[0]].set(smallest).at[spots[1]].set(top_value)


def level_of(rng, dims, cuts, smallest, largest):
    def one(dim, parts):
        draws = jax.random.uniform(jax.random.fold_in(jax.random.fold_in(rng, 6), dim), (parts,), jnp.float32, smallest / len(cuts), largest / len(cuts))
        return jnp.repeat(jnp.exp(draws), dims[dim] // parts).reshape((-1,) + (1,) * (len(dims) - dim - 1))

    level = one(*cuts[0])
    for cut in cuts[1:]:
        level = level * one(*cut)
    return level


def routed_block(own_key, own, number, rows, count, top, limit, lean):
    ranking = jax.random.permutation(own_key, count)
    crowded, usual = portions_of(count, rows * top, limit, lean, True), portions_of(count, rows * top, limit, lean, False)
    places = jnp.arange(count)

    def named(tallies, offset_by):
        used = int((tallies > 0).sum())
        fixed = max(1, used // 4)
        shifted = fixed + (places - fixed + offset_by * (used - fixed)) % max(1, count - fixed)
        return jnp.zeros((count,), jnp.int32).at[ranking[jnp.where(places < fixed, places, shifted)]].set(jnp.asarray(tallies, jnp.int32))

    tallies = jnp.where(number % 4 == 0, named(crowded, number // 4), named(usual, number - number // 4 - 1))
    mixed = jax.random.permutation(jax.random.fold_in(own, 3), count)
    donor, sink = mixed[0:count // 2 * 2:2], mixed[1:count // 2 * 2:2]
    room = jnp.minimum(tallies[donor] - 1, limit - tallies[sink]) // 2
    room = jnp.where((donor == ranking[0]) | (sink == ranking[0]) | (tallies[sink] == 0), 0, jnp.maximum(room, 0))
    shifted = jax.random.randint(jax.random.fold_in(own, 4), (count // 2,), 0, 1 << 20) % (room + 1)
    tallies = tallies.at[donor].add(-shifted).at[sink].add(shifted)
    items = jnp.searchsorted(jnp.cumsum(tallies), jnp.arange(rows * top), side="right").astype(jnp.int32)
    table = items.reshape(top, rows).T
    table = table[jax.random.permutation(jax.random.fold_in(own, 1), rows)]
    offset_by = jax.random.randint(jax.random.fold_in(own, 2), (rows, 1), 0, top)
    return jnp.take_along_axis(table, (jnp.arange(top)[None, :] + offset_by) % top, axis=1)


def portions_of(amount, total, bound, skew, full):
    weights = [(1 << 20) // math.isqrt(standing ** skew) + 1 for standing in range(1, amount + 1)]
    largest = bound if full else min(bound, max(-(-total // amount), total * weights[0] // sum(weights)))
    least = 1 if total - largest >= amount - 1 else 0
    holding, rest = [largest] + [least] * (amount - 1), total - largest - least * (amount - 1)
    while rest > 0:
        free = [i for i in range(1, amount) if holding[i] < largest] or [i for i in range(1, amount) if holding[i] < bound]
        pool, remaining = sum([weights[i] for i in free]), rest
        for i in free:
            addition = min(bound - holding[i], max(1, remaining * weights[i] // pool), rest)
            holding[i] = holding[i] + addition
            rest = rest - addition
    return np.array(holding)


def bell_draw(own_key, dims, scale, bound, split=(), kind=jnp.bfloat16):
    array = jax.random.normal(own_key, dims, jnp.float32) * scale
    if len(split) > 0:
        array = level_of(own_key, dims, split, -0.22, 0.18) * array
    return jnp.clip(array, min=-bound, max=bound).astype(kind)


def setup_inputs(seed: int = 0) -> dict:
    key_of = jax.random.split(jax.random.key(seed), 15)
    anchor = bell_draw(key_of[0], (3, RAYS), 1.0, 4.0, ((1, 256),), jnp.float32)
    direction = bell_draw(key_of[1], (3, RAYS), 1.0, 4.0, ((1, 256),), jnp.float32)
    seg_start = jnp.clip(4.0 * jax.random.uniform(key_of[2], (CROSS, RAYS), jnp.float32) ** level_of(key_of[2], (CROSS, RAYS), ((1, 256),), -0.2, 0.2), 0.0, 4.0)
    seg_step = jnp.clip(jnp.exp(math.log(0.119628906) - 1.7938024 * jax.random.uniform(key_of[3], (CROSS, RAYS), jnp.float32) ** level_of(key_of[3], (CROSS, RAYS), ((1, 256),), -0.2, 0.2)), 0.019897461, 0.119628906).astype(jnp.bfloat16)
    counts = plant(jax.random.randint(key_of[4], (CROSS, RAYS), 1, SEG + 1), jax.random.fold_in(key_of[4], 1), 1, SEG).astype(jnp.int32)
    routes_keys = jax.random.split(jax.random.fold_in(key_of[5], 1), RAYS // RAYS_DEV)
    routes_turns = jax.random.permutation(jax.random.fold_in(key_of[5], 3), RAYS // RAYS_DEV)
    routes = jax.vmap(lambda own, number: routed_block(jax.random.fold_in(key_of[5], 2), own, number, RAYS_DEV, REGIONS, CROSS, MOST, 2))(routes_keys, routes_turns).reshape((RAYS, CROSS))
    order = jax.vmap(lambda own: jax.random.permutation(own, CROSS))(jax.random.split(key_of[6], RAYS)).reshape((RAYS, CROSS)).astype(jnp.int32)
    target = jnp.clip(1.0 * jax.random.uniform(key_of[7], (3, RAYS), jnp.float32) ** level_of(key_of[7], (3, RAYS), ((1, 256),), -0.2, 0.2), 0.0, 1.0)
    fourier = bell_draw(key_of[8], (3, FOURIER), 1.0, 4.0, (), jnp.float32)
    w_input = bell_draw(key_of[9], (REGIONS, ENC, H), ENC ** -0.5, 0.5, ((0, 32),))
    b_input = bell_draw(key_of[10], (REGIONS, H), 0.5, 3.0, ((0, 32),), jnp.float32)
    w_middle = bell_draw(key_of[11], (REGIONS, H, H), H ** -0.5, 0.375, ((0, 32),))
    b_middle = bell_draw(key_of[12], (REGIONS, H), 0.5, 3.0, ((0, 32),), jnp.float32)
    w_output = bell_draw(key_of[13], (REGIONS, 4, H), H ** -0.5, 0.375, ((0, 32),))
    return dict(anchor=anchor, direction=direction, seg_start=seg_start, seg_step=seg_step, counts=counts, routes=routes, order=order, target=target, fourier=fourier, w_input=w_input, b_input=b_input, w_middle=w_middle, b_middle=b_middle, w_output=w_output)


TWO_PI = 2.0 * math.pi

def encode(orig_x, orig_y, orig_z, dir_x, dir_y, dir_z, starts, strides, fourier):
    offsets = jnp.arange(SEG, dtype=jnp.float32) + 0.5
    ray_depth = starts[..., None] + offsets * strides[..., None]
    pos_x = orig_x[..., None] + ray_depth * dir_x[..., None]
    pos_y = orig_y[..., None] + ray_depth * dir_y[..., None]
    pos_z = orig_z[..., None] + ray_depth * dir_z[..., None]
    phases = TWO_PI * (pos_x[..., None] * fourier[0] + pos_y[..., None] * fourier[1] + pos_z[..., None] * fourier[2])
    return jnp.concatenate([jnp.sin(phases), jnp.cos(phases)], axis=-1).astype(jnp.bfloat16)

def spacing_of(strides, counted):
    offsets = jnp.arange(SEG, dtype=jnp.float32)
    return jnp.where(offsets < counted[..., None], strides[..., None], 0.0)

def silu_slope(values):
    sig_vals = jax.nn.sigmoid(values)
    return sig_vals * (1.0 + values * (1.0 - sig_vals))

def composite(head_out, spacing):
    density = jax.nn.softplus(head_out[..., 0])
    tint_rgb = jax.nn.sigmoid(head_out[..., 1:])
    optical = density * spacing
    before_sum = jnp.cumsum(optical, axis=-1) - optical
    shares = jnp.exp(-before_sum) * (1.0 - jnp.exp(-optical))
    colour = lax.optimization_barrier(jnp.sum(shares[..., None] * tint_rgb, axis=-2))
    passed = jnp.exp(-lax.optimization_barrier(jnp.sum(optical, axis=-1)))
    return jnp.concatenate([colour, passed[..., None]], axis=-1)

def merge_rays(segments, order):
    choose = order[:, :, None] == jnp.arange(CROSS, dtype=jnp.int32)[None, None, :]
    ordered = lax.optimization_barrier(jnp.sum(jnp.where(choose[..., None], segments[:, None, :, :], 0.0), axis=2))
    carried = jnp.ones((segments.shape[0],), jnp.float32)
    summed = jnp.zeros((segments.shape[0], 3), jnp.float32)
    for ordinal in range(CROSS):
        summed = summed + carried[:, None] * ordered[:, ordinal, :3]
        carried = carried * ordered[:, ordinal, 3]
    return summed

def forward_rows(features, w_first, b_first, w_second, b_second, w_head):
    z_first = jnp.dot(features, w_first, preferred_element_type=jnp.float32) + b_first
    h_first = jax.nn.silu(z_first).astype(jnp.bfloat16)
    z_second = jnp.dot(h_first, w_second, preferred_element_type=jnp.float32) + b_second
    h_second = jax.nn.silu(z_second).astype(jnp.bfloat16)
    head_out = jnp.dot(h_second, w_head.T, preferred_element_type=jnp.float32)
    return (z_first, h_first, z_second, h_second, head_out)

def backward_rows(features, z_first, h_first, z_second, h_second, head_cot, w_second, w_head):
    cot_bf16 = head_cot.astype(jnp.bfloat16)
    grad_head = jnp.dot(cot_bf16.T, h_second, preferred_element_type=jnp.float32)
    grad_h2 = jnp.dot(cot_bf16, w_head, preferred_element_type=jnp.float32)
    gz_second = (grad_h2 * silu_slope(z_second)).astype(jnp.bfloat16)
    grad_mid = jnp.dot(h_first.T, gz_second, preferred_element_type=jnp.float32)
    grad_bmid = lax.optimization_barrier(jnp.sum(gz_second.astype(jnp.float32), axis=0))
    grad_h1 = jnp.dot(gz_second, w_second.T, preferred_element_type=jnp.float32)
    gz_first = (grad_h1 * silu_slope(z_first)).astype(jnp.bfloat16)
    grad_in = jnp.dot(features.T, gz_first, preferred_element_type=jnp.float32)
    grad_bin = lax.optimization_barrier(jnp.sum(gz_first.astype(jnp.float32), axis=0))
    return (grad_in, grad_bin, grad_mid, grad_bmid, grad_head)

def reference(anchor, direction, seg_start, seg_step, counts, routes, order, target, fourier, w_input, b_input, w_middle, b_middle, w_output):
    devices = N_REP * N_REGION
    per_dev = RAYS_DEV * CROSS
    dev_slots = devices * MOST
    region_ids = routes.reshape(devices, per_dev)
    earlier = jnp.arange(per_dev)[:, None] > jnp.arange(per_dev)[None, :]

    def rank_of(regs_row):
        return lax.optimization_barrier(jnp.sum((regs_row[:, None] == regs_row[None, :]) & earlier, axis=1)).astype(jnp.int32)
    rank_ids = lax.map(rank_of, region_ids)
    device_ids = jnp.arange(devices, dtype=jnp.int32)[:, None]
    slot_ids = (region_ids * dev_slots + device_ids * MOST + rank_ids).reshape(-1).astype(jnp.int32)

    def spread(values):
        return jnp.broadcast_to(values[:, None], (RAYS, CROSS)).reshape(-1)
    geometry = jnp.stack([spread(anchor[0]), spread(anchor[1]), spread(anchor[2]), spread(direction[0]), spread(direction[1]), spread(direction[2]), seg_start.T.reshape(-1), seg_step.T.astype(jnp.float32).reshape(-1), counts.T.reshape(-1).astype(jnp.float32)], axis=1)
    slot_table = jnp.zeros((REGIONS * dev_slots, 9), jnp.float32).at[slot_ids].set(geometry)
    slot_table = slot_table.reshape(REGIONS, dev_slots, 9)

    def region_forward(packed):
        geo_rows, w_first, b_first, w_second, b_second, w_head = packed
        features = encode(geo_rows[:, 0], geo_rows[:, 1], geo_rows[:, 2], geo_rows[:, 3], geo_rows[:, 4], geo_rows[:, 5], geo_rows[:, 6], geo_rows[:, 7], fourier)
        spacing = spacing_of(geo_rows[:, 7], geo_rows[:, 8])
        flat_feat = features.reshape(-1, features.shape[-1])
        outs_all = forward_rows(flat_feat, w_first, b_first, w_second, b_second, w_head)
        head_out = outs_all[4].reshape(dev_slots, SEG, 4)
        return (flat_feat, spacing, outs_all, head_out)

    def region_outputs(packed):
        flat_feat, spacing, outs_all, head_out = region_forward(packed)
        return composite(head_out, spacing)
    weights_all = (w_input, b_input, w_middle, b_middle, w_output)
    seg_table = lax.map(region_outputs, (slot_table,) + weights_all).reshape(REGIONS * dev_slots, 4)
    seg_entries = seg_table[slot_ids].reshape(RAYS, CROSS, 4)
    colour, merge_back = jax.vjp(lambda seg_vals: merge_rays(seg_vals, order), seg_entries)
    rendered = colour.T
    seg_cot = merge_back((colour - target.T) / LOSS_DIV)[0].reshape(-1, 4)
    cot_table = jnp.zeros((REGIONS * dev_slots, 4), jnp.float32).at[slot_ids].set(seg_cot)
    cot_table = cot_table.reshape(REGIONS, dev_slots, 4)

    def region_grads(packed):
        seg_rows = packed[0]
        flat_feat, spacing, outs_all, head_out = region_forward(packed[1:])
        _, comp_back = jax.vjp(lambda head_vals: composite(head_vals, spacing), head_out)
        head_cot = comp_back(seg_rows)[0].reshape(-1, 4)
        z_first, h_first, z_second, h_second, _ = outs_all
        return backward_rows(flat_feat, z_first, h_first, z_second, h_second, head_cot, packed[4], packed[6])
    grads = lax.map(region_grads, (cot_table, slot_table) + weights_all)
    return (rendered, grads[0], grads[1], grads[2], grads[3], grads[4])
```

```python
import functools
import math

import jax
import jax.numpy as jnp
import numpy as np
from jax import lax
from jax.experimental import pallas as pl
from jax.experimental.pallas import tpu as pltpu
from jax.sharding import PartitionSpec as P

SEG = 16
CH = 64
F32, BF16 = jnp.float32, jnp.bfloat16
VM = pltpu.VMEM
NT = (((1,), (1,)), ((), ()))
TN = (((0,), (0,)), ((), ()))


def _sine_coeffs():
    k = np.arange(64)
    y = 0.125 + 0.125 * np.cos(math.pi * (k + 0.5) / 64)
    r = np.sqrt(y)
    poly = np.polynomial.chebyshev.Chebyshev.interpolate(
        lambda q: np.sin(2 * math.pi * np.sqrt(q)) / np.sqrt(q), 5, domain=[1e-12, 0.25]
    )
    return [float(c) for c in poly.convert(kind=np.polynomial.Polynomial).coef]


COEF = _sine_coeffs()


def sine_turns(u):
    r = u - jnp.round(u)
    y = r * r
    p = jnp.full_like(y, COEF[5])
    for c in COEF[4::-1]:
        p = p * y + c
    return p * r


def split3(x):
    hi = x.astype(BF16)
    rest = x - hi.astype(F32)
    mid = rest.astype(BF16)
    low = (rest - mid.astype(F32)).astype(BF16)
    return hi, mid, low


def pick(a, b, dims, split_first):
    if split_first:
        parts = [lax.dot_general(x, b, dims, preferred_element_type=F32) for x in split3(a)]
    else:
        parts = [lax.dot_general(a, x, dims, preferred_element_type=F32) for x in split3(b)]
    return (parts[0] + parts[1]) + parts[2]


def iota(shape, dim):
    return lax.broadcasted_iota(jnp.int32, shape, dim)


def dispatch(slot, vals, groups):
    entries = slot.shape[1]
    dest = (iota((groups, entries), 0) == slot // 32).astype(F32).astype(BF16)
    lane = iota((32, entries), 0) == slot % 32
    rows = jnp.concatenate([jnp.where(lane, v, 0.0) for v in vals], axis=0)
    return pick(dest, rows, NT, False)


def send_kernel(anchor, direction, start, step, counts, routes, geo_out, slot_out):
    groups = geo_out.shape[0]
    regs = jnp.concatenate([routes[k : k + 1, :] for k in range(4)], axis=1)
    entries = regs.shape[1]
    regions = groups * 4
    hot = (iota((regions, entries), 0) == regs).astype(F32)
    upper = (iota((entries, entries), 0) < iota((entries, entries), 1)).astype(F32).astype(BF16)
    earlier = jnp.dot(hot.astype(BF16), upper, preferred_element_type=F32)
    rank = jnp.sum(hot * earlier, axis=0, keepdims=True).astype(jnp.int32)
    slot = regs * 8 + rank
    slot_out[...] = slot
    stp = step[...].astype(F32)
    cnt = counts[...].astype(F32)
    rows = []
    for c in range(3):
        rows.append(
            jnp.concatenate(
                [anchor[c : c + 1, :] + start[k : k + 1, :] * direction[c : c + 1, :] for k in range(4)],
                axis=1,
            )
        )
    rows.append(jnp.concatenate([cnt[k : k + 1, :] for k in range(4)], axis=1))
    for c in range(3):
        rows.append(
            jnp.concatenate([stp[k : k + 1, :] * direction[c : c + 1, :] for k in range(4)], axis=1)
        )
    rows.append(jnp.concatenate([stp[k : k + 1, :] for k in range(4)], axis=1))
    geo_out[:, 0, :] = dispatch(slot, rows[:4], groups)
    geo_out[:, 1, :] = dispatch(slot, rows[4:], groups)


def region_plan(geo0, s):
    groups = geo0.shape[0]
    lanes = iota((groups, 128), 1)
    live = jnp.where((lanes // 8 == 12 + s) & (geo0 > 0.5), 1.0, 0.0)
    num = jnp.sum(live, axis=1, keepdims=True)
    before = iota((groups, groups), 1) < iota((groups, groups), 0)
    first = jnp.dot(
        before.astype(F32).astype(BF16),
        jnp.broadcast_to(num, (groups, 128)).astype(BF16),
        preferred_element_type=F32,
    )[:, :1]
    return num, first


def chunk_map(num, first, base):
    groups = num.shape[0]
    j = (iota((groups, 128), 1) % CH + base).astype(F32)
    src = jnp.where((j >= first) & (j < first + num), 1.0, 0.0)
    place = (j[:1, :] - jnp.sum(src * first, axis=0, keepdims=True)).astype(jnp.int32)
    return src.astype(BF16), place


def chunk_take(arr, src, place, s):
    full = pick(arr, src, TN, True)
    mask = iota((8, 128), 0) == place
    rows = []
    for w in range(4):
        part = jnp.zeros((8, 128), F32)
        for t in range(4):
            at = w * 32 + t * 8
            part = jnp.where(s == t, full[at : at + 8, :], part)
        rows.append(jnp.sum(jnp.where(mask, part, 0.0), axis=0, keepdims=True))
    return rows


def encode(head, rest, fcol):
    px, py, pz, count = head
    dx, dy, dz, step = rest
    fx, fy, fz, turn = (fcol[:, c : c + 1] for c in range(4))
    begin = px * fx + py * fy + pz * fz
    slope = dx * fx + dy * fy + dz * fz
    half = (iota((1, 128), 1) // CH).astype(F32)
    begin = begin + (half + 0.5) * slope + turn
    begin = (begin - jnp.round(begin)).T
    slope = (slope - jnp.round(slope)).T
    feats = [sine_turns(begin + (2.0 * p) * slope).astype(BF16) for p in range(8)]
    return jnp.concatenate(feats, axis=0)


def sigmoid(v):
    return 0.5 * jnp.tanh(0.5 * v) + 0.5


def layers(feat, w_in, b_in, w_mid, b_mid):
    z1 = jnp.dot(feat, w_in, preferred_element_type=F32) + b_in
    s1 = sigmoid(z1)
    h1 = z1 * s1
    h1b = h1.astype(BF16)
    z2 = jnp.dot(h1b, w_mid, preferred_element_type=F32) + b_mid
    s2 = sigmoid(z2)
    h2 = z2 * s2
    return s1, h1, h1b, s2, h2, h2.astype(BF16)


def both(row):
    return row + pltpu.roll(row, CH, 1)


def segment_terms(head_t, count, step):
    upper_half = iota((1, 128), 1) >= CH
    half = (iota((1, 128), 1) // CH).astype(F32)
    total = jnp.zeros((1, 128), F32)
    terms = []
    for p in range(8):
        blk = head_t[:, p * 128 : (p + 1) * 128]
        spacing = jnp.where(2.0 * p + half < count, step, 0.0)
        top = blk[:1, :]
        density = jnp.maximum(top, 0.0) + jnp.log1p(jnp.exp(-jnp.abs(top)))
        optical = density * spacing
        other = pltpu.roll(optical, CH, 1)
        before = total + jnp.where(upper_half, other, 0.0)
        total = total + optical + other
        reach = jnp.exp(-before)
        keep = jnp.exp(-optical)
        terms.append((spacing, reach, keep, reach * (1.0 - keep), sigmoid(blk)))
    return terms, jnp.exp(-total)


def forward_kernel(geo, fcol, w_in, b_in, w_mid, b_mid, w_head, res_out):
    s = pl.program_id(0)
    geo0, geo1 = geo[:, 0, :], geo[:, 1, :]
    groups = geo0.shape[0]
    num, first = region_plan(geo0, s)
    amount = jnp.sum(num).astype(jnp.int32)

    @pl.when(s == 0)
    def _():
        res_out[...] = jnp.zeros_like(res_out)

    def step_of(i, carry):
        src, place = chunk_map(num, first, i * CH)
        head = chunk_take(geo0, src, place, s)
        rest = chunk_take(geo1, src, place, s)
        feat = encode(head, rest, fcol)
        h2b = layers(feat, w_in[0], b_in[0], w_mid[0], b_mid[0])[5]
        head_t = lax.dot_general(w_head[0], h2b, NT, preferred_element_type=F32)[:8]
        terms, passed = segment_terms(head_t, head[3], rest[3])
        colour = jnp.zeros((8, 128), F32)
        for _, _, _, share, tint in terms:
            colour = colour + share * tint
        colour = both(colour)
        first_half = iota((1, 128), 1) < CH
        mask = (iota((8, 128), 0) == place) & first_half
        blocks = []
        for w in range(4):
            row = passed if w == 3 else colour[w + 1 : w + 2, :]
            hit = jnp.where(mask, row, 0.0)
            for t in range(4):
                blocks.append(jnp.where(s == t, hit, 0.0))
        z = jnp.concatenate(blocks, axis=0)
        res_out[...] += pick(src, z, NT, False)
        return carry

    lax.fori_loop(0, (amount + CH - 1) // CH, step_of, 0)


def merge_kernel(slot, order, target, res, rendered_out, cot_out):
    groups = res.shape[0]
    sl = slot[...]
    entries = sl.shape[1]
    dest = (iota((groups, entries), 0) == sl // 32).astype(F32).astype(BF16)
    full = pick(res[...], dest, TN, True)
    lane = iota((32, entries), 0) == sl % 32
    vals = [
        jnp.sum(jnp.where(lane, full[w * 32 : (w + 1) * 32, :], 0.0), axis=0, keepdims=True)
        for w in range(4)
    ]
    rays = entries // 4
    seg = [[vals[w][:, k * rays : (k + 1) * rays] for w in range(4)] for k in range(4)]
    which = [order[j : j + 1, :] for j in range(4)]
    ordered = []
    for j in range(4):
        ordered.append(
            [sum(jnp.where(which[j] == k, seg[k][w], 0.0) for k in range(4)) for w in range(4)]
        )
    carried = [jnp.ones((1, rays), F32)]
    colour = [jnp.zeros((1, rays), F32)] * 3
    for j in range(4):
        colour = [colour[c] + carried[j] * ordered[j][c] for c in range(3)]
        carried.append(carried[j] * ordered[j][3])
    for c in range(3):
        rendered_out[c : c + 1, :] = colour[c]
    grad = [(colour[c] - target[c : c + 1, :]) * (1.0 / 16.0) for c in range(3)]
    cots = [None] * 4
    tail = jnp.zeros((1, rays), F32)
    for j in (3, 2, 1, 0):
        cots[j] = [carried[j] * g for g in grad] + [carried[j] * tail]
        tail = sum(ordered[j][c] * grad[c] for c in range(3)) + ordered[j][3] * tail
    rows = []
    for w in range(4):
        rows.append(
            jnp.concatenate(
                [sum(jnp.where(which[j] == k, cots[j][w], 0.0) for j in range(4)) for k in range(4)],
                axis=1,
            )
        )
    cot_out[...] = dispatch(sl, rows, groups)


def backward_kernel(geo, cot, fcol, w_in, b_in, w_mid, b_mid, w_head, out, g_in, g_mid, g_bin, g_bmid, g_head):
    s = pl.program_id(0)
    geo0, geo1 = geo[:, 0, :], geo[:, 1, :]
    num, first = region_plan(geo0, s)
    amount = jnp.sum(num).astype(jnp.int32)
    for ref in (g_in, g_mid, g_bin, g_bmid, g_head):
        ref[...] = jnp.zeros_like(ref)

    def step_of(i, carry):
        src, place = chunk_map(num, first, i * CH)
        head = chunk_take(geo0, src, place, s)
        rest = chunk_take(geo1, src, place, s)
        given = chunk_take(cot[...], src, place, s)
        feat = encode(head, rest, fcol)
        s1, h1, h1b, s2, h2, h2b = layers(feat, w_in[0], b_in[0], w_mid[0], b_mid[0])
        head_t = lax.dot_general(w_head[0], h2b, NT, preferred_element_type=F32)[:8]
        terms, passed = segment_terms(head_t, head[3], rest[3])
        zero = jnp.zeros((1, 128), F32)
        paint = jnp.concatenate([zero, given[0], given[1], given[2], zero, zero, zero, zero], axis=0)
        lower_half = iota((1, 128), 1) < CH
        after = given[3] * passed
        top_row = iota((8, 128), 0) == 0
        cots = [None] * 8
        for p in range(7, -1, -1):
            spacing, reach, keep, share, tint = terms[p]
            weight = jnp.sum(paint * tint, axis=0, keepdims=True)
            gain = share * weight
            other = pltpu.roll(gain, CH, 1)
            later = after + jnp.where(lower_half, other, 0.0)
            after = after + gain + other
            g_opt = (reach * keep * weight - later) * spacing
            cots[p] = jnp.where(top_row, g_opt * tint, paint * share * tint * (1.0 - tint))
        cot_t = jnp.concatenate(cots, axis=1)
        cot_t = jnp.concatenate([cot_t, jnp.zeros_like(cot_t)], axis=0)
        cot_b = cot_t.astype(BF16)
        g_head[...] += jnp.dot(cot_b, h2b, preferred_element_type=F32)
        gh2 = lax.dot_general(cot_b, w_head[0], TN, preferred_element_type=F32)
        gz2 = gh2 * (s2 + h2 * (1.0 - s2))
        gz2b = gz2.astype(BF16)
        g_mid[...] += lax.dot_general(h1b, gz2b, TN, preferred_element_type=F32)
        g_bmid[...] += jnp.sum(gz2.reshape(-1, 8, gz2.shape[1]), axis=0)
        gh1 = lax.dot_general(gz2b, w_mid[0], NT, preferred_element_type=F32)
        gz1 = gh1 * (s1 + h1 * (1.0 - s1))
        gz1b = gz1.astype(BF16)
        g_in[...] += lax.dot_general(feat, gz1b, TN, preferred_element_type=F32)
        g_bin[...] += jnp.sum(gz1.reshape(-1, 8, gz1.shape[1]), axis=0)
        return carry

    lax.fori_loop(0, (amount + CH - 1) // CH, step_of, 0)
    enc = g_in.shape[0]
    hid = g_mid.shape[0]
    out[0, 0:enc, :] = g_in[...].astype(BF16)
    out[0, enc : enc + hid, :] = g_mid[...].astype(BF16)
    row = iota(g_head.shape, 0)
    b1 = jnp.sum(g_bin[...], axis=0, keepdims=True)
    b2 = jnp.sum(g_bmid[...], axis=0, keepdims=True)
    tail = jnp.where(row == 8, b1, jnp.where(row == 9, b2, g_head[...]))
    out[0, enc + hid : enc + hid + 16, :] = tail.astype(BF16)
    out[0, enc + hid + 16 : enc + hid + 32, :] = jnp.zeros_like(tail).astype(BF16)


def total_kernel(parts, out):
    acc = parts[0].astype(F32)
    for i in range(1, parts.shape[0]):
        acc = acc + parts[i].astype(F32)
    out[...] = acc.astype(BF16)


def spread_kernel(packed, o_in, o_bin, o_mid, o_bmid, o_head):
    regions, enc, hid = o_in.shape
    for s in range(regions):
        o_in[s] = packed[s, 0:enc, :].astype(F32)
        o_mid[s] = packed[s, enc : enc + hid, :].astype(F32)
        tail = packed[s, enc + hid : enc + hid + 16, :].astype(F32)
        o_head[s] = tail[0:4, :]
        o_bin[s : s + 1, :] = tail[8:9, :]
        o_bmid[s : s + 1, :] = tail[9:10, :]


def call(kernel, outs, *args, **more):
    return pl.pallas_call(
        kernel,
        out_shape=outs,
        compiler_params=pltpu.CompilerParams(vmem_limit_bytes=56 * 2**20),
        **more,
    )(*args)


def struct(*shape, dtype=F32):
    return jax.ShapeDtypeStruct(shape, dtype)


def a2a(x, axis):
    return lax.all_to_all(x, axis, split_axis=0, concat_axis=0, tiled=True)


def body(
    anchor, direction, seg_start, seg_step, counts, routes, order, target,
    fourier, w_input, b_input, w_middle, b_middle, w_output,
):
    groups = lax.axis_size("region")
    reps = lax.axis_size("rep")
    subs, enc, hid = w_input.shape
    rays = anchor.shape[1]
    freqs = fourier.shape[1]
    fcol = jnp.zeros((enc, 128), F32)
    fcol = fcol.at[:, 0:3].set(jnp.concatenate([fourier.T, fourier.T], axis=0))
    fcol = fcol.at[freqs:, 3].set(0.25)
    w_head = jnp.pad(w_output, ((0, 0), (0, 12), (0, 0)))
    b_in, b_mid = b_input[:, None, :], b_middle[:, None, :]

    geo_send, slot = call(
        send_kernel,
        (struct(groups, 2, 128), struct(1, rays * 4, dtype=jnp.int32)),
        anchor, direction, seg_start, seg_step, counts, routes.T,
    )
    geo = a2a(geo_send, "region")

    def whole(*shape):
        return pl.BlockSpec(shape, lambda s: (0,) * len(shape))

    def per_region(*shape):
        return pl.BlockSpec((1,) + shape, lambda s: (s,) + (0,) * len(shape))

    net_specs = [
        whole(enc, 128), per_region(enc, hid), per_region(1, hid), per_region(hid, hid),
        per_region(1, hid), per_region(16, hid),
    ]
    net = (fcol, w_input, b_in, w_middle, b_mid, w_head)
    res = call(
        forward_kernel,
        struct(groups, 128),
        geo, *net,
        grid=(subs,),
        in_specs=[whole(groups, 2, 128)] + net_specs,
        out_specs=whole(groups, 128),
    )
    res_back = a2a(res[:, None, :], "region")[:, 0, :]
    rendered, cot_send = call(
        merge_kernel,
        (struct(3, rays), struct(groups, 128)),
        slot, order.T, target, res_back,
    )
    cot = a2a(cot_send[:, None, :], "region")[:, 0, :]
    rows = enc + hid + 32
    packed = call(
        backward_kernel,
        struct(subs, rows, hid, dtype=BF16),
        geo, cot, *net,
        grid=(subs,),
        in_specs=[whole(groups, 2, 128), whole(groups, 128)] + net_specs,
        out_specs=per_region(rows, hid),
        scratch_shapes=[
            VM((enc, hid), F32), VM((hid, hid), F32), VM((8, hid), F32), VM((8, hid), F32), VM((16, hid), F32),
        ],
    )
    parts = a2a(packed.reshape(reps, subs * rows // reps, hid), "rep")
    mine = call(total_kernel, struct(subs * rows // reps, hid, dtype=BF16), parts)
    full = lax.all_gather(mine, "rep", axis=0, tiled=True).reshape(subs, rows, hid)
    grads = call(
        spread_kernel,
        (struct(subs, enc, hid), struct(subs, hid), struct(subs, hid, hid), struct(subs, hid), struct(subs, 4, hid)),
        full,
    )
    return (rendered, *grads)


def solution(mesh):
    rays, own = ("rep", "region"), "region"
    return jax.shard_map(
        body,
        mesh=mesh,
        in_specs=(
            P(None, rays), P(None, rays), P(None, rays), P(None, rays), P(None, rays),
            P(rays, None), P(rays, None), P(None, rays), P(),
            P(own, None, None), P(own, None), P(own, None, None), P(own, None), P(own, None, None),
        ),
        out_specs=(
            P(None, rays), P(own, None, None), P(own, None), P(own, None, None), P(own, None), P(own, None, None),
        ),
        check_vma=False,
    )
```

```python
import functools
import math

import jax
import jax.numpy as jnp
import numpy as np
from jax import lax
from jax.experimental import pallas as pl
from jax.experimental.pallas import tpu as pltpu
from jax.sharding import PartitionSpec as P

SEG = 16
PAD = 32
CH = 64
F32, BF16 = jnp.float32, jnp.bfloat16
VM = pltpu.VMEM
NT = (((1,), (1,)), ((), ()))
TN = (((0,), (0,)), ((), ()))


def _sine_coeffs():
    k = np.arange(64)
    y = 0.125 + 0.125 * np.cos(math.pi * (k + 0.5) / 64)
    r = np.sqrt(y)
    poly = np.polynomial.chebyshev.Chebyshev.interpolate(
        lambda q: np.sin(2 * math.pi * np.sqrt(q)) / np.sqrt(q), 5, domain=[1e-12, 0.25]
    )
    return [float(c) for c in poly.convert(kind=np.polynomial.Polynomial).coef]


COEF = _sine_coeffs()


def sine_turns(u):
    r = u - jnp.round(u)
    y = r * r
    p = jnp.full_like(y, COEF[5])
    for c in COEF[4::-1]:
        p = p * y + c
    return p * r


def split3(x):
    hi = x.astype(BF16)
    rest = x - hi.astype(F32)
    mid = rest.astype(BF16)
    low = (rest - mid.astype(F32)).astype(BF16)
    return hi, mid, low


def pick(a, b, dims, split_first):
    if split_first:
        parts = [lax.dot_general(x, b, dims, preferred_element_type=F32) for x in split3(a)]
    else:
        parts = [lax.dot_general(a, x, dims, preferred_element_type=F32) for x in split3(b)]
    return (parts[0] + parts[1]) + parts[2]


def iota(shape, dim):
    return lax.broadcasted_iota(jnp.int32, shape, dim)


def dispatch(slot, vals, groups):
    entries = slot.shape[1]
    dest = (iota((groups, entries), 0) == slot // 32).astype(F32).astype(BF16)
    lane = iota((32, entries), 0) == slot % 32
    rows = jnp.concatenate([jnp.where(lane, v, 0.0) for v in vals], axis=0)
    return pick(dest, rows, NT, False)


def send_kernel(anchor, direction, start, step, counts, routes, geo_out, slot_out):
    groups = geo_out.shape[0]
    regs = jnp.concatenate([routes[k : k + 1, :] for k in range(4)], axis=1)
    entries = regs.shape[1]
    regions = groups * 4
    hot = (iota((regions, entries), 0) == regs).astype(F32)
    upper = (iota((entries, entries), 0) < iota((entries, entries), 1)).astype(F32).astype(BF16)
    earlier = jnp.dot(hot.astype(BF16), upper, preferred_element_type=F32)
    rank = jnp.sum(hot * earlier, axis=0, keepdims=True).astype(jnp.int32)
    slot = regs * 8 + rank
    slot_out[...] = slot
    stp = step[...].astype(F32)
    cnt = counts[...].astype(F32)
    rows = []
    for c in range(3):
        rows.append(
            jnp.concatenate(
                [anchor[c : c + 1, :] + start[k : k + 1, :] * direction[c : c + 1, :] for k in range(4)],
                axis=1,
            )
        )
    rows.append(jnp.concatenate([cnt[k : k + 1, :] for k in range(4)], axis=1))
    for c in range(3):
        rows.append(
            jnp.concatenate([stp[k : k + 1, :] * direction[c : c + 1, :] for k in range(4)], axis=1)
        )
    rows.append(jnp.concatenate([stp[k : k + 1, :] for k in range(4)], axis=1))
    geo_out[:, 0, :] = dispatch(slot, rows[:4], groups)
    geo_out[:, 1, :] = dispatch(slot, rows[4:], groups)


def region_plan(geo0, s):
    groups = geo0.shape[0]
    lanes = iota((groups, 128), 1)
    live = jnp.where((lanes // 8 == 12 + s) & (geo0 > 0.5), 1.0, 0.0)
    num = jnp.sum(live, axis=1, keepdims=True)
    before = iota((groups, groups), 1) < iota((groups, groups), 0)
    first = jnp.dot(
        before.astype(F32).astype(BF16),
        jnp.broadcast_to(num, (groups, 128)).astype(BF16),
        preferred_element_type=F32,
    )[:, :1]
    return num, first


def region_map(num, first):
    groups = num.shape[0]
    wide = groups * 8 * 2
    lane = iota((groups, wide), 1)
    j = (lane // 128 * CH + lane % CH).astype(F32)
    src = jnp.where((j >= first) & (j < first + num), 1.0, 0.0)
    place = (j[:1, :] - jnp.sum(src * first, axis=0, keepdims=True)).astype(jnp.int32)
    return src.astype(BF16), place


def region_take(arr, src, place, s):
    full = pick(arr, src, TN, True)
    mask = iota((8, src.shape[1]), 0) == place
    return [
        jnp.sum(jnp.where(mask, full[w * 32 + s * 8 : w * 32 + s * 8 + 8, :], 0.0), axis=0, keepdims=True)
        for w in range(4)
    ]


def find(n, ends):
    s = sum((n >= e).astype(jnp.int32) for e in ends[:-1])
    start = jnp.int32(0)
    for e in ends[:-1]:
        start = jnp.where(n >= e, e, start)
    return s, n - start


def encode(head, rest, fcol):
    px, py, pz, count = head
    dx, dy, dz, step = rest
    fx, fy, fz, turn = (fcol[:, c : c + 1] for c in range(4))
    begin = px * fx + py * fy + pz * fz
    slope = dx * fx + dy * fy + dz * fz
    half = (iota((1, 128), 1) // CH).astype(F32)
    begin = begin + (half + 0.5) * slope + turn
    begin = (begin - jnp.round(begin)).T
    slope = (slope - jnp.round(slope)).T
    slope = slope + slope
    feats = []
    for p in range(8):
        feats.append(sine_turns(begin).astype(BF16))
        begin = begin + slope
    return jnp.concatenate(feats, axis=0)


def columns_of(fourier):
    both_halves = jnp.concatenate([fourier, fourier], axis=1)
    width = both_halves.shape[1]
    turn = jnp.where(iota((1, width), 1) >= width // 2, 0.25, 0.0)
    return jnp.concatenate([both_halves, turn, jnp.zeros((width - 4, width), F32)], axis=0).T


def head_rows(w):
    w = w.astype(F32)
    return jnp.concatenate([w, jnp.zeros((12, w.shape[1]), F32)], axis=0)


def sigmoid(v):
    return 0.5 * jnp.tanh(0.5 * v) + 0.5


def layer(x, w_half, b_half):
    v = jnp.dot(x, w_half, preferred_element_type=F32) + b_half
    t = jnp.tanh(v)
    q = v * t
    return (v + q).astype(BF16), ((1.0 + t) * ((1.0 + v) - q)).astype(BF16)


def both(row):
    return row + pltpu.roll(row, CH, 1)


def segment_terms(head_t, count, step):
    upper_half = iota((1, 128), 1) >= CH
    half = (iota((1, 128), 1) // CH).astype(F32)
    total = jnp.zeros((1, 128), F32)
    terms = []
    for p in range(8):
        blk = head_t[:, p * 128 : (p + 1) * 128]
        spacing = jnp.where(2.0 * p + half < count, step, 0.0)
        top = blk[:1, :]
        density = jnp.maximum(top, 0.0) + jnp.log1p(jnp.exp(-jnp.abs(top)))
        optical = density * spacing
        other = pltpu.roll(optical, CH, 1)
        before = total + jnp.where(upper_half, other, 0.0)
        total = total + optical + other
        reach = jnp.exp(-before)
        keep = jnp.exp(-optical)
        terms.append((spacing, reach, keep, reach * (1.0 - keep), sigmoid(blk)))
    return terms, jnp.exp(-total)


def forward_kernel(
    geo, fourier, w_in, b_in, w_mid, b_mid, w_head, res_out, rows_out, heads_out, chunks_out, kept_out,
    seg_rows, w_in_half, w_mid_half, heads, kept, sem,
):
    fcol = columns_of(fourier[...])
    geo0, geo1 = geo[:, 0, :], geo[:, 1, :]
    enc, hid = w_in.shape[1:]
    subs = w_in.shape[0]
    maps, ends = [], []
    total = jnp.int32(0)
    for s in range(subs):
        num, first = region_plan(geo0, s)
        amount = (jnp.sum(num).astype(jnp.int32) + CH - 1) // CH
        chunks_out[s] = amount
        w_in_half[s] = w_in[s] * 0.5
        w_mid_half[s] = w_mid[s] * 0.5
        heads[s] = head_rows(w_head[s]).astype(BF16)
        total = total + amount
        ends.append(total)
        src, place = region_map(num, first)
        maps.append((src, place))
        rows_out[s] = jnp.concatenate(
            region_take(geo0, src, place, s) + region_take(geo1, src, place, s), axis=0
        )
    seg_rows[...] = jnp.zeros_like(seg_rows)
    per = rows_out.shape[2] // 128

    def copy(slot, at):
        return pltpu.make_async_copy(kept.at[slot], kept_out.at[at], sem.at[slot])

    def step_of(n, carry):
        s, i = find(n, ends)
        slot = n % 2

        @pl.when(n >= 2)
        def _():
            copy(slot, 0).wait()

        lanes = pl.ds(pl.multiple_of(i * 128, 128), 128)
        rows = rows_out[s, :, lanes]
        rows = [rows[w : w + 1, :] for w in range(8)]
        feat = encode(rows[:4], rows[4:], fcol)
        h1b, slope1 = layer(feat, w_in_half[s], b_in[pl.ds(s, 1), :] * 0.5)
        h2b, slope2 = layer(h1b, w_mid_half[s], b_mid[pl.ds(s, 1), :] * 0.5)
        at = 0
        for part in (feat, h1b, h2b, slope1, slope2):
            kept[slot, :, at : at + part.shape[1]] = part
            at += part.shape[1]
        copy(slot, s * per + i).start()
        head_t = lax.dot_general(heads[s], h2b, NT, preferred_element_type=F32)[:8]
        heads_out[s * per + i] = head_t
        terms, passed = segment_terms(head_t, rows[3], rows[7])
        colour = jnp.zeros((8, 128), F32)
        for _, _, _, share, tint in terms:
            colour = colour + share * tint
        colour = both(colour)
        seg_rows[s, :, lanes] = jnp.where(iota((8, 128), 0) == 0, passed, colour)
        return carry

    lax.fori_loop(0, total, step_of, 0)

    @pl.when(total >= 1)
    def _():
        copy((total - 1) % 2, 0).wait()

    @pl.when(total >= 2)
    def _():
        copy(total % 2, 0).wait()

    acc = jnp.zeros(res_out.shape, F32)
    for s in range(subs):
        src, place = maps[s]
        wide = src.shape[1]
        mask = (iota((8, wide), 0) == place) & (iota((8, wide), 1) % 128 < CH)
        none = jnp.zeros((8, wide), F32)
        blocks = []
        for w in range(4):
            row = (w + 1) % 4
            hit = jnp.where(mask, seg_rows[s, row : row + 1, :], 0.0)
            blocks += [hit if t == s else none for t in range(4)]
        acc = acc + pick(src, jnp.concatenate(blocks, axis=0), NT, False)
    res_out[...] = acc


def merge_kernel(slot, order, target, res, rendered_out, cot_out):
    groups = res.shape[0]
    sl = slot[...]
    entries = sl.shape[1]
    dest = (iota((groups, entries), 0) == sl // 32).astype(F32).astype(BF16)
    full = pick(res[...], dest, TN, True)
    lane = iota((32, entries), 0) == sl % 32
    vals = [
        jnp.sum(jnp.where(lane, full[w * 32 : (w + 1) * 32, :], 0.0), axis=0, keepdims=True)
        for w in range(4)
    ]
    rays = entries // 4
    seg = [[vals[w][:, k * rays : (k + 1) * rays] for w in range(4)] for k in range(4)]
    which = [order[j : j + 1, :] for j in range(4)]
    ordered = []
    for j in range(4):
        ordered.append(
            [sum(jnp.where(which[j] == k, seg[k][w], 0.0) for k in range(4)) for w in range(4)]
        )
    carried = [jnp.ones((1, rays), F32)]
    colour = [jnp.zeros((1, rays), F32)] * 3
    for j in range(4):
        colour = [colour[c] + carried[j] * ordered[j][c] for c in range(3)]
        carried.append(carried[j] * ordered[j][3])
    for c in range(3):
        rendered_out[c : c + 1, :] = colour[c]
    grad = [(colour[c] - target[c : c + 1, :]) * (1.0 / 16.0) for c in range(3)]
    cots = [None] * 4
    tail = jnp.zeros((1, rays), F32)
    for j in (3, 2, 1, 0):
        cots[j] = [carried[j] * g for g in grad] + [carried[j] * tail]
        tail = sum(ordered[j][c] * grad[c] for c in range(3)) + ordered[j][3] * tail
    rows = []
    for w in range(4):
        rows.append(
            jnp.concatenate(
                [sum(jnp.where(which[j] == k, cots[j][w], 0.0) for j in range(4)) for k in range(4)],
                axis=1,
            )
        )
    cot_out[...] = dispatch(sl, rows, groups)


def backward_kernel(
    chunks, geo, cot, rows_in, heads, w_mid, w_head, kept_in, out,
    given, w_mid_half, head_half, g_in, g_mid, g_bin, g_bmid, g_head, kept, sem,
):
    geo0, cots_in = geo[:, 0, :], cot[...]
    subs, enc, hid = g_in.shape
    per = rows_in.shape[2] // 128
    ends = []
    total = jnp.int32(0)
    for t in range(subs):
        total = total + chunks[t]
        ends.append(total)

    def copy(slot, at):
        return pltpu.make_async_copy(kept_in.at[at], kept.at[slot], sem.at[slot])

    def fetch(n):
        t, i = find(n, ends)
        copy(n % 2, t * per + i).start()

    @pl.when(total >= 1)
    def _():
        fetch(jnp.int32(0))

    for t in range(subs):
        src, place = region_map(*region_plan(geo0, t))
        rows = region_take(cots_in, src, place, t)
        w_mid_half[t] = w_mid[t] * 0.5
        head_half[t] = (head_rows(w_head[t]) * 0.5).astype(BF16)
        given[t] = jnp.concatenate(rows + rows, axis=0)
    for ref in (g_in, g_mid, g_bin, g_bmid, g_head):
        ref[...] = jnp.zeros_like(ref)

    def step_of(n, carry):
        t, i = find(n, ends)
        slot = n % 2

        @pl.when(n + 1 < total)
        def _():
            fetch(n + 1)

        lanes = pl.ds(pl.multiple_of(i * 128, 128), 128)
        rows = rows_in[t, :, lanes]
        cot_rows = given[t, :, lanes]
        terms, passed = segment_terms(heads[t * per + i], rows[3:4, :], rows[7:8, :])
        channel = iota((8, 128), 0)
        paint = jnp.zeros((8, 128), F32)
        for c in range(3):
            paint = jnp.where(channel == c + 1, cot_rows[c : c + 1, :], paint)
        lower_half = iota((1, 128), 1) < CH
        after = cot_rows[3:4, :] * passed
        top_row = channel == 0
        cots = [None] * 8
        for p in range(7, -1, -1):
            spacing, reach, keep, share, tint = terms[p]
            weight = jnp.sum(paint * tint, axis=0, keepdims=True)
            gain = share * weight
            other = pltpu.roll(gain, CH, 1)
            later = after + jnp.where(lower_half, other, 0.0)
            after = after + gain + other
            g_opt = (reach * keep * weight - later) * spacing
            cots[p] = jnp.where(top_row, g_opt * tint, paint * share * tint * (1.0 - tint))
        cot_t = jnp.concatenate(cots, axis=1)
        cot_b = jnp.concatenate([cot_t, jnp.zeros_like(cot_t)], axis=0).astype(BF16)
        copy(slot, 0).wait()
        feat = kept[slot, :, 0:enc]
        h1b = kept[slot, :, enc : enc + hid]
        h2b = kept[slot, :, enc + hid : enc + 2 * hid]
        slope1 = kept[slot, :, enc + 2 * hid : enc + 3 * hid].astype(F32)
        slope2 = kept[slot, :, enc + 3 * hid : enc + 4 * hid].astype(F32)
        g_head[t] += jnp.dot(cot_b, h2b, preferred_element_type=F32)
        gz2 = lax.dot_general(cot_b, head_half[t], TN, preferred_element_type=F32) * slope2
        gz2b = gz2.astype(BF16)
        g_mid[t] += lax.dot_general(h1b, gz2b, TN, preferred_element_type=F32)
        g_bmid[t] += jnp.sum(gz2.reshape(-1, 8, hid), axis=0)
        gz1 = lax.dot_general(gz2b, w_mid_half[t], NT, preferred_element_type=F32) * slope1
        gz1b = gz1.astype(BF16)
        g_in[t] += lax.dot_general(feat, gz1b, TN, preferred_element_type=F32)
        g_bin[t] += jnp.sum(gz1.reshape(-1, 8, hid), axis=0)
        return carry

    lax.fori_loop(0, total, step_of, 0)
    row = iota((16, hid), 0)
    for t in range(subs):
        out[t, 0:enc, :] = g_in[t].astype(BF16)
        out[t, enc : enc + hid, :] = g_mid[t].astype(BF16)
        b1 = jnp.sum(g_bin[t], axis=0, keepdims=True)
        b2 = jnp.sum(g_bmid[t], axis=0, keepdims=True)
        tail = jnp.where(row == 8, b1, jnp.where(row == 9, b2, g_head[t]))
        out[t, enc + hid : enc + hid + 16, :] = tail.astype(BF16)
        out[t, enc + hid + 16 :, :] = jnp.zeros((PAD - 16, hid), BF16)


def total_kernel(parts, out):
    acc = parts[0].astype(F32)
    for i in range(1, parts.shape[0]):
        acc = acc + parts[i].astype(F32)
    out[...] = acc.astype(BF16)


def spread_kernel(packed, o_in, o_bin, o_mid, o_bmid, o_head):
    regions, enc, hid = o_in.shape
    for s in range(regions):
        o_in[s] = packed[s, 0:enc, :].astype(F32)
        o_mid[s] = packed[s, enc : enc + hid, :].astype(F32)
        tail = packed[s, enc + hid : enc + hid + 16, :].astype(F32)
        o_head[s] = tail[0:4, :]
        o_bin[s : s + 1, :] = tail[8:9, :]
        o_bmid[s : s + 1, :] = tail[9:10, :]


def call(kernel, outs, *args, **more):
    return pl.pallas_call(
        kernel,
        out_shape=outs,
        compiler_params=pltpu.CompilerParams(vmem_limit_bytes=56 * 2**20),
        **more,
    )(*args)


def struct(*shape, dtype=F32):
    return jax.ShapeDtypeStruct(shape, dtype)


def a2a(x, axis):
    return lax.all_to_all(x, axis, split_axis=0, concat_axis=0, tiled=True)


def body(
    anchor, direction, seg_start, seg_step, counts, routes, order, target,
    fourier, w_input, b_input, w_middle, b_middle, w_output,
):
    groups = lax.axis_size("region")
    reps = lax.axis_size("rep")
    subs, enc, hid = w_input.shape
    rays = anchor.shape[1]
    geo_send, slot = call(
        send_kernel,
        (struct(groups, 2, 128), struct(1, rays * 4, dtype=jnp.int32)),
        anchor, direction, seg_start, seg_step, counts, routes.T,
    )
    geo = a2a(geo_send, "region")

    wide = groups * 16
    chunk_cap = subs * groups * 8 // CH
    width = enc + 4 * hid
    any_spec, vm_spec = pl.BlockSpec(memory_space=pl.ANY), pl.BlockSpec(memory_space=pltpu.VMEM)
    sm_spec = pl.BlockSpec(memory_space=pltpu.SMEM)
    res, seg_geo, heads, chunks, kept = call(
        forward_kernel,
        (
            struct(groups, 128), struct(subs, 8, wide), struct(chunk_cap, 8, CH * SEG),
            struct(subs, dtype=jnp.int32), struct(chunk_cap, CH * SEG, width, dtype=BF16),
        ),
        geo, fourier, w_input, b_input, w_middle, b_middle, w_output,
        out_specs=(vm_spec, vm_spec, vm_spec, sm_spec, any_spec),
        scratch_shapes=[
            VM((subs, 8, wide), F32), VM((subs, enc, hid), BF16), VM((subs, hid, hid), BF16), VM((subs, 16, hid), BF16),
            VM((2, CH * SEG, width), BF16), pltpu.SemaphoreType.DMA((2,)),
        ],
    )
    res_back = a2a(res[:, None, :], "region")[:, 0, :]
    rendered, cot_send = call(
        merge_kernel,
        (struct(3, rays), struct(groups, 128)),
        slot, order.T, target, res_back,
    )
    cot = a2a(cot_send[:, None, :], "region")[:, 0, :]
    rows = enc + hid + PAD
    packed = call(
        backward_kernel,
        struct(subs, rows, hid, dtype=BF16),
        chunks, geo, cot, seg_geo, heads, w_middle, w_output, kept,
        in_specs=[sm_spec] + [vm_spec] * 6 + [any_spec],
        scratch_shapes=[
            VM((subs, 8, wide), F32), VM((subs, hid, hid), BF16), VM((subs, 16, hid), BF16),
            VM((subs, enc, hid), F32), VM((subs, hid, hid), F32), VM((subs, 8, hid), F32), VM((subs, 8, hid), F32),
            VM((subs, 16, hid), F32), VM((2, CH * SEG, width), BF16), pltpu.SemaphoreType.DMA((2,)),
        ],
    )
    parts = a2a(packed.reshape(reps, subs * rows // reps, hid), "rep")
    mine = call(total_kernel, struct(*parts.shape[1:], dtype=BF16), parts)
    full = lax.all_gather(mine, "rep", axis=0, tiled=True).reshape(subs, rows, hid)
    grads = call(
        spread_kernel,
        (struct(subs, enc, hid), struct(subs, hid), struct(subs, hid, hid), struct(subs, hid), struct(subs, 4, hid)),
        full,
    )
    return (rendered, *grads)


def solution(mesh):
    rays, own = ("rep", "region"), "region"
    return jax.shard_map(
        body,
        mesh=mesh,
        in_specs=(
            P(None, rays), P(None, rays), P(None, rays), P(None, rays), P(None, rays),
            P(rays, None), P(rays, None), P(None, rays), P(),
            P(own, None, None), P(own, None), P(own, None, None), P(own, None), P(own, None, None),
        ),
        out_specs=(
            P(None, rays), P(own, None, None), P(own, None), P(own, None, None), P(own, None), P(own, None, None),
        ),
        check_vma=False,
    )
```

```python
import functools
import math

import jax
import jax.numpy as jnp
import numpy as np
from jax import lax
from jax.experimental import pallas as pl
from jax.experimental.pallas import tpu as pltpu
from jax.sharding import PartitionSpec as P

SEG = 16
BLOCK = 256
BLOCKB = 512
PAD = 32
CH = 64
F32, BF16 = jnp.float32, jnp.bfloat16
VM = pltpu.VMEM
NT = (((1,), (1,)), ((), ()))
TN = (((0,), (0,)), ((), ()))


def _sine_coeffs():
    k = np.arange(64)
    y = 0.125 + 0.125 * np.cos(math.pi * (k + 0.5) / 64)
    r = np.sqrt(y)
    poly = np.polynomial.chebyshev.Chebyshev.interpolate(
        lambda q: np.sin(2 * math.pi * np.sqrt(q)) / np.sqrt(q), 5, domain=[1e-12, 0.25]
    )
    return [float(c) for c in poly.convert(kind=np.polynomial.Polynomial).coef]


COEF = _sine_coeffs()


def sine_turns(u):
    r = u - jnp.round(u)
    y = r * r
    p = jnp.full_like(y, COEF[5])
    for c in COEF[4::-1]:
        p = p * y + c
    return p * r


def split3(x):
    hi = x.astype(BF16)
    rest = x - hi.astype(F32)
    mid = rest.astype(BF16)
    low = (rest - mid.astype(F32)).astype(BF16)
    return hi, mid, low


def pick(a, b, dims, split_first):
    if split_first:
        parts = [lax.dot_general(x, b, dims, preferred_element_type=F32) for x in split3(a)]
    else:
        parts = [lax.dot_general(a, x, dims, preferred_element_type=F32) for x in split3(b)]
    return (parts[0] + parts[1]) + parts[2]


def iota(shape, dim):
    return lax.broadcasted_iota(jnp.int32, shape, dim)


def dispatch(slot, vals, groups):
    entries = slot.shape[1]
    dest = (iota((groups, entries), 0) == slot // 32).astype(F32).astype(BF16)
    lane = iota((32, entries), 0) == slot % 32
    rows = jnp.concatenate([jnp.where(lane, v, 0.0) for v in vals], axis=0)
    return pick(dest, rows, NT, False)


def send_kernel(anchor, direction, start, step, counts, routes, geo_out, slot_out):
    groups = geo_out.shape[0]
    regs = jnp.concatenate([routes[k : k + 1, :] for k in range(4)], axis=1)
    entries = regs.shape[1]
    regions = groups * 4
    hot = (iota((regions, entries), 0) == regs).astype(F32)
    upper = (iota((entries, entries), 0) < iota((entries, entries), 1)).astype(F32).astype(BF16)
    earlier = jnp.dot(hot.astype(BF16), upper, preferred_element_type=F32)
    rank = jnp.sum(hot * earlier, axis=0, keepdims=True).astype(jnp.int32)
    slot = regs * 8 + rank
    slot_out[...] = slot
    stp = step[...].astype(F32)
    cnt = counts[...].astype(F32)
    rows = []
    for c in range(3):
        rows.append(
            jnp.concatenate(
                [anchor[c : c + 1, :] + start[k : k + 1, :] * direction[c : c + 1, :] for k in range(4)],
                axis=1,
            )
        )
    rows.append(jnp.concatenate([cnt[k : k + 1, :] for k in range(4)], axis=1))
    for c in range(3):
        rows.append(
            jnp.concatenate([stp[k : k + 1, :] * direction[c : c + 1, :] for k in range(4)], axis=1)
        )
    rows.append(jnp.concatenate([stp[k : k + 1, :] for k in range(4)], axis=1))
    geo_out[:, 0, :] = dispatch(slot, rows[:4], groups)
    geo_out[:, 1, :] = dispatch(slot, rows[4:], groups)


def region_plan(geo0, s):
    groups = geo0.shape[0]
    lanes = iota((groups, 128), 1)
    live = jnp.where((lanes // 8 == 12 + s) & (geo0 > 0.5), 1.0, 0.0)
    num = jnp.sum(live, axis=1, keepdims=True)
    before = iota((groups, groups), 1) < iota((groups, groups), 0)
    first = jnp.dot(
        before.astype(F32).astype(BF16),
        jnp.broadcast_to(num, (groups, 128)).astype(BF16),
        preferred_element_type=F32,
    )[:, :1]
    return num, first


def region_map(num, first):
    groups = num.shape[0]
    wide = groups * 8 * 2
    lane = iota((groups, wide), 1)
    j = (lane // 128 * CH + lane % CH).astype(F32)
    src = jnp.where((j >= first) & (j < first + num), 1.0, 0.0)
    place = (j[:1, :] - jnp.sum(src * first, axis=0, keepdims=True)).astype(jnp.int32)
    return src.astype(BF16), place


def region_take(arrs, src, place, s):
    own = jnp.concatenate([a[w * 32 + s * 8 : w * 32 + s * 8 + 8, :] for a in arrs for w in range(4)], axis=0)
    found = jnp.dot(jnp.concatenate(split3(own), axis=0), src, preferred_element_type=F32)
    rows = own.shape[0]
    full = (found[:rows] + found[rows : 2 * rows]) + found[2 * rows :]
    mask = iota((8, src.shape[1]), 0) == place
    return jnp.concatenate(
        [
            jnp.sum(jnp.where(mask, full[r : r + 8, :], 0.0), axis=0, keepdims=True)
            for r in range(0, rows, 8)
        ],
        axis=0,
    )


def find(n, ends):
    s = sum((n >= e).astype(jnp.int32) for e in ends[:-1])
    start = jnp.int32(0)
    for e in ends[:-1]:
        start = jnp.where(n >= e, e, start)
    return s, n - start


def encode(head, rest, fcol):
    px, py, pz, count = head
    dx, dy, dz, step = rest
    fx, fy, fz, turn = (fcol[:, c : c + 1] for c in range(4))
    begin = px * fx + py * fy + pz * fz
    slope = dx * fx + dy * fy + dz * fz
    half = (iota((1, 128), 1) // CH).astype(F32)
    begin = begin + (half + 0.5) * slope + turn
    begin = (begin - jnp.round(begin)).T
    slope = (slope - jnp.round(slope)).T
    slope = slope + slope
    feats = []
    for p in range(8):
        feats.append(sine_turns(begin).astype(BF16))
        begin = begin + slope
    return feats


def columns_of(fourier):
    both_halves = jnp.concatenate([fourier, fourier], axis=1)
    width = both_halves.shape[1]
    turn = jnp.where(iota((1, width), 1) >= width // 2, 0.25, 0.0)
    return jnp.concatenate([both_halves, turn, jnp.zeros((width - 4, width), F32)], axis=0).T


def head_rows(w):
    w = w.astype(F32)
    return jnp.concatenate([w, jnp.zeros((12, w.shape[1]), F32)], axis=0)


def sigmoid(v):
    return 0.5 * jnp.tanh(0.5 * v) + 0.5


def layer(x, w_half, b_half):
    v = jnp.dot(x, w_half, preferred_element_type=F32) + b_half
    t = jnp.tanh(v)
    q = v * t
    return (v + q).astype(BF16), ((1.0 + t) * ((1.0 + v) - q)).astype(BF16)


def both(row):
    return row + pltpu.roll(row, CH, 1)


def segment_terms(head_t, count, step):
    upper_half = iota((1, 128), 1) >= CH
    half = (iota((1, 128), 1) // CH).astype(F32)
    total = jnp.zeros((1, 128), F32)
    terms = []
    for p in range(8):
        blk = head_t[:, p * 128 : (p + 1) * 128]
        spacing = jnp.where(2.0 * p + half < count, step, 0.0)
        top = blk[:1, :]
        density = jnp.maximum(top, 0.0) + jnp.log1p(jnp.exp(-jnp.abs(top)))
        optical = density * spacing
        other = pltpu.roll(optical, CH, 1)
        before = total + jnp.where(upper_half, other, 0.0)
        total = total + optical + other
        reach = jnp.exp(-before)
        keep = jnp.exp(-optical)
        terms.append((spacing, reach, keep, reach * (1.0 - keep), sigmoid(blk)))
    return terms, jnp.exp(-total)


def forward_kernel(
    geo, fourier, w_in, b_in, w_mid, b_mid, w_head, res_out, rows_out, heads_out, chunks_out, kept_out,
    seg_rows, w_in_half, w_mid_half, heads, kept, sem,
):
    fcol = columns_of(fourier[...])
    geo0, geo1 = geo[:, 0, :], geo[:, 1, :]
    enc, hid = w_in.shape[1:]
    subs = w_in.shape[0]
    turned = (geo0.T, geo1.T)
    maps, ends = [], []
    total = jnp.int32(0)
    for s in range(subs):
        num, first = region_plan(geo0, s)
        amount = (jnp.sum(num).astype(jnp.int32) + CH - 1) // CH
        chunks_out[s] = amount
        w_in_half[s] = w_in[s] * 0.5
        w_mid_half[s] = w_mid[s] * 0.5
        heads[s] = head_rows(w_head[s]).astype(BF16)
        total = total + amount
        ends.append(total)
        src, place = region_map(num, first)
        maps.append((src, place))
        rows_out[s] = region_take(turned, src, place, s)
    seg_rows[...] = jnp.zeros_like(seg_rows)
    per = rows_out.shape[2] // 128

    def copy(slot, at):
        return pltpu.make_async_copy(kept.at[slot], kept_out.at[at], sem.at[slot])

    def step_of(n, carry):
        s, i = find(n, ends)
        slot = n % 2

        @pl.when(n >= 2)
        def _():
            copy(slot, 0).wait()

        lanes = pl.ds(pl.multiple_of(i * 128, 128), 128)
        rows = rows_out[s, :, lanes]
        rows = [rows[w : w + 1, :] for w in range(8)]
        feats = encode(rows[:4], rows[4:], fcol)
        w1, w2 = w_in_half[s], w_mid_half[s]
        b1, b2 = b_in[pl.ds(s, 1), :] * 0.5, b_mid[pl.ds(s, 1), :] * 0.5
        h2_blocks = []
        for q in range(0, CH * SEG, BLOCK):
            feat = jnp.concatenate(feats[q // 128 : (q + BLOCK) // 128], axis=0)
            h1b, slope1 = layer(feat, w1, b1)
            h2b, slope2 = layer(h1b, w2, b2)
            at = 0
            for part in (feat, h1b, h2b, slope1, slope2):
                kept[slot, q : q + BLOCK, at : at + part.shape[1]] = part
                at += part.shape[1]
            h2_blocks.append(h2b)
        h2b = jnp.concatenate(h2_blocks, axis=0)
        copy(slot, s * per + i).start()
        head_t = lax.dot_general(heads[s], h2b, NT, preferred_element_type=F32)[:8]
        heads_out[s * per + i] = head_t
        terms, passed = segment_terms(head_t, rows[3], rows[7])
        colour = jnp.zeros((8, 128), F32)
        for _, _, _, share, tint in terms:
            colour = colour + share * tint
        colour = both(colour)
        seg_rows[s, :, lanes] = jnp.where(iota((8, 128), 0) == 0, passed, colour)
        return carry

    lax.fori_loop(0, total, step_of, 0)

    @pl.when(total >= 1)
    def _():
        copy((total - 1) % 2, 0).wait()

    @pl.when(total >= 2)
    def _():
        copy(total % 2, 0).wait()

    found = []
    for s in range(subs):
        src, place = maps[s]
        wide = src.shape[1]
        mask = (iota((8, wide), 0) == place) & (iota((8, wide), 1) % 128 < CH)
        own = jnp.concatenate(
            [jnp.where(mask, seg_rows[s, r : r + 1, :], 0.0) for r in (1, 2, 3, 0)], axis=0
        )
        full = lax.dot_general(jnp.concatenate(split3(own), axis=0), src, NT, preferred_element_type=F32)
        found.append((full[0:32] + full[32:64]) + full[64:96])
    res_out[...] = jnp.concatenate(
        [found[s][w * 8 : w * 8 + 8, :] for w in range(4) for s in range(subs)], axis=0
    ).T


def merge_kernel(slot, order, target, res, rendered_out, cot_out):
    groups = res.shape[0]
    sl = slot[...]
    entries = sl.shape[1]
    dest = (iota((groups, entries), 0) == sl // 32).astype(F32).astype(BF16)
    full = pick(res[...], dest, TN, True)
    lane = iota((32, entries), 0) == sl % 32
    vals = [
        jnp.sum(jnp.where(lane, full[w * 32 : (w + 1) * 32, :], 0.0), axis=0, keepdims=True)
        for w in range(4)
    ]
    rays = entries // 4
    seg = [[vals[w][:, k * rays : (k + 1) * rays] for w in range(4)] for k in range(4)]
    which = [order[j : j + 1, :] for j in range(4)]
    ordered = []
    for j in range(4):
        ordered.append(
            [sum(jnp.where(which[j] == k, seg[k][w], 0.0) for k in range(4)) for w in range(4)]
        )
    carried = [jnp.ones((1, rays), F32)]
    colour = [jnp.zeros((1, rays), F32)] * 3
    for j in range(4):
        colour = [colour[c] + carried[j] * ordered[j][c] for c in range(3)]
        carried.append(carried[j] * ordered[j][3])
    for c in range(3):
        rendered_out[c : c + 1, :] = colour[c]
    grad = [(colour[c] - target[c : c + 1, :]) * (1.0 / 16.0) for c in range(3)]
    cots = [None] * 4
    tail = jnp.zeros((1, rays), F32)
    for j in (3, 2, 1, 0):
        cots[j] = [carried[j] * g for g in grad] + [carried[j] * tail]
        tail = sum(ordered[j][c] * grad[c] for c in range(3)) + ordered[j][3] * tail
    rows = []
    for w in range(4):
        rows.append(
            jnp.concatenate(
                [sum(jnp.where(which[j] == k, cots[j][w], 0.0) for j in range(4)) for k in range(4)],
                axis=1,
            )
        )
    cot_out[...] = dispatch(sl, rows, groups)


def backward_kernel(
    chunks, geo, cot, rows_in, heads, w_mid, w_head, kept_in, out,
    given, w_mid_half, head_half, g_in, g_mid, g_bin, g_bmid, g_head, kept, sem,
):
    geo0, turned = geo[:, 0, :], cot[...].T
    subs, enc, hid = g_in.shape
    per = rows_in.shape[2] // 128
    ends = []
    total = jnp.int32(0)
    for t in range(subs):
        total = total + chunks[t]
        ends.append(total)

    def copy(slot, at):
        return pltpu.make_async_copy(kept_in.at[at], kept.at[slot], sem.at[slot])

    def fetch(n):
        t, i = find(n, ends)
        copy(n % 2, t * per + i).start()

    @pl.when(total >= 1)
    def _():
        fetch(jnp.int32(0))

    for t in range(subs):
        src, place = region_map(*region_plan(geo0, t))
        rows = region_take((turned,), src, place, t)
        w_mid_half[t] = w_mid[t] * 0.5
        head_half[t] = (head_rows(w_head[t]) * 0.5).astype(BF16)
        given[t] = jnp.concatenate([rows, rows], axis=0)
    for ref in (g_in, g_mid, g_bin, g_bmid, g_head):
        ref[...] = jnp.zeros_like(ref)

    def step_of(n, carry):
        t, i = find(n, ends)
        slot = n % 2

        @pl.when(n + 1 < total)
        def _():
            fetch(n + 1)

        lanes = pl.ds(pl.multiple_of(i * 128, 128), 128)
        rows = rows_in[t, :, lanes]
        cot_rows = given[t, :, lanes]
        terms, passed = segment_terms(heads[t * per + i], rows[3:4, :], rows[7:8, :])
        channel = iota((8, 128), 0)
        paint = jnp.zeros((8, 128), F32)
        for c in range(3):
            paint = jnp.where(channel == c + 1, cot_rows[c : c + 1, :], paint)
        lower_half = iota((1, 128), 1) < CH
        after = cot_rows[3:4, :] * passed
        top_row = channel == 0
        cots = [None] * 8
        for p in range(7, -1, -1):
            spacing, reach, keep, share, tint = terms[p]
            weight = jnp.sum(paint * tint, axis=0, keepdims=True)
            gain = share * weight
            other = pltpu.roll(gain, CH, 1)
            later = after + jnp.where(lower_half, other, 0.0)
            after = after + gain + other
            g_opt = (reach * keep * weight - later) * spacing
            cots[p] = jnp.where(top_row, g_opt * tint, paint * share * tint * (1.0 - tint))
        cot_t = jnp.concatenate(cots, axis=1)
        cot_b = jnp.concatenate([cot_t, jnp.zeros_like(cot_t)], axis=0).astype(BF16)
        copy(slot, 0).wait()
        feat = kept[slot, :, 0:enc]
        h1b = kept[slot, :, enc : enc + hid]
        h2b = kept[slot, :, enc + hid : enc + 2 * hid]
        g_head[t] += jnp.dot(cot_b, h2b, preferred_element_type=F32)
        cot_rows_b = cot_b.astype(F32).T.astype(BF16)
        gz2_blocks, gz1_blocks = [], []
        sum1 = sum2 = jnp.zeros((8, hid), F32)
        for q in range(0, CH * SEG, BLOCKB):
            slope2 = kept[slot, q : q + BLOCKB, enc + 3 * hid : enc + 4 * hid].astype(F32)
            gz2 = jnp.dot(cot_rows_b[q : q + BLOCKB], head_half[t], preferred_element_type=F32) * slope2
            gz2b = gz2.astype(BF16)
            sum2 = sum2 + jnp.sum(gz2.reshape(-1, 8, hid), axis=0)
            slope1 = kept[slot, q : q + BLOCKB, enc + 2 * hid : enc + 3 * hid].astype(F32)
            gz1 = lax.dot_general(gz2b, w_mid_half[t], NT, preferred_element_type=F32) * slope1
            sum1 = sum1 + jnp.sum(gz1.reshape(-1, 8, hid), axis=0)
            gz2_blocks.append(gz2b)
            gz1_blocks.append(gz1.astype(BF16))
        gz2b, gz1b = jnp.concatenate(gz2_blocks, axis=0), jnp.concatenate(gz1_blocks, axis=0)
        g_mid[t] += lax.dot_general(h1b, gz2b, TN, preferred_element_type=F32)
        g_bmid[t] += sum2
        g_bin[t] += sum1
        g_in[t] += lax.dot_general(feat, gz1b, TN, preferred_element_type=F32)
        return carry

    lax.fori_loop(0, total, step_of, 0)
    row = iota((16, hid), 0)
    for t in range(subs):
        out[t, 0:enc, :] = g_in[t].astype(BF16)
        out[t, enc : enc + hid, :] = g_mid[t].astype(BF16)
        b1 = jnp.sum(g_bin[t], axis=0, keepdims=True)
        b2 = jnp.sum(g_bmid[t], axis=0, keepdims=True)
        tail = jnp.where(row == 8, b1, jnp.where(row == 9, b2, g_head[t]))
        out[t, enc + hid : enc + hid + 16, :] = tail.astype(BF16)
        out[t, enc + hid + 16 :, :] = jnp.zeros((PAD - 16, hid), BF16)


def total_kernel(parts, out):
    acc = parts[0].astype(F32)
    for i in range(1, parts.shape[0]):
        acc = acc + parts[i].astype(F32)
    out[...] = acc.astype(BF16)


def spread_kernel(packed, o_in, o_bin, o_mid, o_bmid, o_head):
    regions, enc, hid = o_in.shape
    for s in range(regions):
        o_in[s] = packed[s, 0:enc, :].astype(F32)
        o_mid[s] = packed[s, enc : enc + hid, :].astype(F32)
        tail = packed[s, enc + hid : enc + hid + 16, :].astype(F32)
        o_head[s] = tail[0:4, :]
        o_bin[s : s + 1, :] = tail[8:9, :]
        o_bmid[s : s + 1, :] = tail[9:10, :]


def call(kernel, outs, *args, **more):
    return pl.pallas_call(
        kernel,
        out_shape=outs,
        compiler_params=pltpu.CompilerParams(vmem_limit_bytes=56 * 2**20),
        **more,
    )(*args)


def struct(*shape, dtype=F32):
    return jax.ShapeDtypeStruct(shape, dtype)


def a2a(x, axis):
    return lax.all_to_all(x, axis, split_axis=0, concat_axis=0, tiled=True)


def body(
    anchor, direction, seg_start, seg_step, counts, routes, order, target,
    fourier, w_input, b_input, w_middle, b_middle, w_output,
):
    groups = lax.axis_size("region")
    reps = lax.axis_size("rep")
    subs, enc, hid = w_input.shape
    rays = anchor.shape[1]
    geo_send, slot = call(
        send_kernel,
        (struct(groups, 2, 128), struct(1, rays * 4, dtype=jnp.int32)),
        anchor, direction, seg_start, seg_step, counts, routes.T,
    )
    geo = a2a(geo_send, "region")

    wide = groups * 16
    chunk_cap = subs * groups * 8 // CH
    width = enc + 4 * hid
    any_spec, vm_spec = pl.BlockSpec(memory_space=pl.ANY), pl.BlockSpec(memory_space=pltpu.VMEM)
    sm_spec = pl.BlockSpec(memory_space=pltpu.SMEM)
    res, seg_geo, heads, chunks, kept = call(
        forward_kernel,
        (
            struct(groups, 128), struct(subs, 8, wide), struct(chunk_cap, 8, CH * SEG),
            struct(subs, dtype=jnp.int32), struct(chunk_cap, CH * SEG, width, dtype=BF16),
        ),
        geo, fourier, w_input, b_input, w_middle, b_middle, w_output,
        out_specs=(vm_spec, vm_spec, vm_spec, sm_spec, any_spec),
        scratch_shapes=[
            VM((subs, 8, wide), F32), VM((subs, enc, hid), BF16), VM((subs, hid, hid), BF16), VM((subs, 16, hid), BF16),
            VM((2, CH * SEG, width), BF16), pltpu.SemaphoreType.DMA((2,)),
        ],
    )
    res_back = a2a(res[:, None, :], "region")[:, 0, :]
    rendered, cot_send = call(
        merge_kernel,
        (struct(3, rays), struct(groups, 128)),
        slot, order.T, target, res_back,
    )
    cot = a2a(cot_send[:, None, :], "region")[:, 0, :]
    rows = enc + hid + PAD
    packed = call(
        backward_kernel,
        struct(subs, rows, hid, dtype=BF16),
        chunks, geo, cot, seg_geo, heads, w_middle, w_output, kept,
        in_specs=[sm_spec] + [vm_spec] * 6 + [any_spec],
        scratch_shapes=[
            VM((subs, 8, wide), F32), VM((subs, hid, hid), BF16), VM((subs, 16, hid), BF16),
            VM((subs, enc, hid), F32), VM((subs, hid, hid), F32), VM((subs, 8, hid), F32), VM((subs, 8, hid), F32),
            VM((subs, 16, hid), F32), VM((2, CH * SEG, width), BF16), pltpu.SemaphoreType.DMA((2,)),
        ],
    )
    parts = a2a(packed.reshape(reps, subs * rows // reps, hid), "rep")
    mine = call(total_kernel, struct(*parts.shape[1:], dtype=BF16), parts)
    full = lax.all_gather(mine, "rep", axis=0, tiled=True).reshape(subs, rows, hid)
    grads = call(
        spread_kernel,
        (struct(subs, enc, hid), struct(subs, hid), struct(subs, hid, hid), struct(subs, hid), struct(subs, 4, hid)),
        full,
    )
    return (rendered, *grads)


def solution(mesh):
    rays, own = ("rep", "region"), "region"
    return jax.shard_map(
        body,
        mesh=mesh,
        in_specs=(
            P(None, rays), P(None, rays), P(None, rays), P(None, rays), P(None, rays),
            P(rays, None), P(rays, None), P(None, rays), P(),
            P(own, None, None), P(own, None), P(own, None, None), P(own, None), P(own, None, None),
        ),
        out_specs=(
            P(None, rays), P(own, None, None), P(own, None), P(own, None, None), P(own, None), P(own, None, None),
        ),
        check_vma=False,
    )
```

```python
import functools
import math

import jax
import jax.numpy as jnp
import numpy as np
from jax import lax
from jax.experimental import pallas as pl
from jax.experimental.pallas import tpu as pltpu
from jax.sharding import PartitionSpec as P

SEG = 16
BLOCK = 256
BLOCKB = 512
PAD = 32
CH = 64
F32, BF16 = jnp.float32, jnp.bfloat16
VM = pltpu.VMEM
NT = (((1,), (1,)), ((), ()))
TN = (((0,), (0,)), ((), ()))


def _sine_coeffs():
    k = np.arange(64)
    y = 0.125 + 0.125 * np.cos(math.pi * (k + 0.5) / 64)
    r = np.sqrt(y)
    poly = np.polynomial.chebyshev.Chebyshev.interpolate(
        lambda q: np.sin(2 * math.pi * np.sqrt(q)) / np.sqrt(q), 5, domain=[1e-12, 0.25]
    )
    return [float(c) for c in poly.convert(kind=np.polynomial.Polynomial).coef]


COEF = _sine_coeffs()


def sine_turns(u):
    r = u - jnp.round(u)
    y = r * r
    p = jnp.full_like(y, COEF[5])
    for c in COEF[4::-1]:
        p = p * y + c
    return p * r


def split3(x):
    hi = x.astype(BF16)
    rest = x - hi.astype(F32)
    mid = rest.astype(BF16)
    low = (rest - mid.astype(F32)).astype(BF16)
    return hi, mid, low


def pick(a, b, dims, split_first):
    if split_first:
        parts = [lax.dot_general(x, b, dims, preferred_element_type=F32) for x in split3(a)]
    else:
        parts = [lax.dot_general(a, x, dims, preferred_element_type=F32) for x in split3(b)]
    return (parts[0] + parts[1]) + parts[2]


def iota(shape, dim):
    return lax.broadcasted_iota(jnp.int32, shape, dim)


def dispatch(slot, vals, groups):
    entries = slot.shape[1]
    dest = (iota((groups, entries), 0) == slot // 32).astype(F32).astype(BF16)
    lane = iota((32, entries), 0) == slot % 32
    rows = jnp.concatenate([jnp.where(lane, v, 0.0) for v in vals], axis=0)
    return pick(dest, rows, NT, False)


def send_kernel(anchor, direction, start, step, counts, routes, geo_out, slot_out):
    groups = geo_out.shape[0]
    regs = jnp.concatenate([routes[k : k + 1, :] for k in range(4)], axis=1)
    entries = regs.shape[1]
    regions = groups * 4
    hot = (iota((regions, entries), 0) == regs).astype(F32)
    upper = (iota((entries, entries), 0) < iota((entries, entries), 1)).astype(F32).astype(BF16)
    earlier = jnp.dot(hot.astype(BF16), upper, preferred_element_type=F32)
    rank = jnp.sum(hot * earlier, axis=0, keepdims=True).astype(jnp.int32)
    slot = regs * 8 + rank
    slot_out[...] = slot
    stp = step[...].astype(F32)
    cnt = counts[...].astype(F32)
    rows = []
    for c in range(3):
        rows.append(
            jnp.concatenate(
                [anchor[c : c + 1, :] + start[k : k + 1, :] * direction[c : c + 1, :] for k in range(4)],
                axis=1,
            )
        )
    rows.append(jnp.concatenate([cnt[k : k + 1, :] for k in range(4)], axis=1))
    for c in range(3):
        rows.append(
            jnp.concatenate([stp[k : k + 1, :] * direction[c : c + 1, :] for k in range(4)], axis=1)
        )
    rows.append(jnp.concatenate([stp[k : k + 1, :] for k in range(4)], axis=1))
    geo_out[:, 0, :] = dispatch(slot, rows[:4], groups)
    geo_out[:, 1, :] = dispatch(slot, rows[4:], groups)


def region_plan(geo0, s):
    groups = geo0.shape[0]
    lanes = iota((groups, 128), 1)
    live = jnp.where((lanes // 8 == 12 + s) & (geo0 > 0.5), 1.0, 0.0)
    num = jnp.sum(live, axis=1, keepdims=True)
    before = iota((groups, groups), 1) < iota((groups, groups), 0)
    first = jnp.dot(
        before.astype(F32).astype(BF16),
        jnp.broadcast_to(num, (groups, 128)).astype(BF16),
        preferred_element_type=F32,
    )[:, :1]
    return num, first


def region_map(num, first):
    groups = num.shape[0]
    wide = groups * 8 * 2
    lane = iota((groups, wide), 1)
    j = (lane // 128 * CH + lane % CH).astype(F32)
    src = jnp.where((j >= first) & (j < first + num), 1.0, 0.0)
    place = (j[:1, :] - jnp.sum(src * first, axis=0, keepdims=True)).astype(jnp.int32)
    return src.astype(BF16), place


def region_take(arrs, src, place, s):
    own = jnp.concatenate([a[w * 32 + s * 8 : w * 32 + s * 8 + 8, :] for a in arrs for w in range(4)], axis=0)
    found = jnp.dot(jnp.concatenate(split3(own), axis=0), src, preferred_element_type=F32)
    rows = own.shape[0]
    full = (found[:rows] + found[rows : 2 * rows]) + found[2 * rows :]
    mask = iota((8, src.shape[1]), 0) == place
    return jnp.concatenate(
        [
            jnp.sum(jnp.where(mask, full[r : r + 8, :], 0.0), axis=0, keepdims=True)
            for r in range(0, rows, 8)
        ],
        axis=0,
    )


def find(n, ends):
    s = sum((n >= e).astype(jnp.int32) for e in ends[:-1])
    start = jnp.int32(0)
    for e in ends[:-1]:
        start = jnp.where(n >= e, e, start)
    return s, n - start


def encode(head, rest, fcol):
    px, py, pz, count = head
    dx, dy, dz, step = rest
    fx, fy, fz, turn = (fcol[:, c : c + 1] for c in range(4))
    begin = px * fx + py * fy + pz * fz
    slope = dx * fx + dy * fy + dz * fz
    half = (iota((1, 128), 1) // CH).astype(F32)
    begin = begin + (half + 0.5) * slope + turn
    begin = (begin - jnp.round(begin)).T
    slope = (slope - jnp.round(slope)).T
    slope = slope + slope
    feats = []
    for p in range(8):
        feats.append(sine_turns(begin).astype(BF16))
        begin = begin + slope
    return feats


def columns_of(fourier):
    both_halves = jnp.concatenate([fourier, fourier], axis=1)
    width = both_halves.shape[1]
    turn = jnp.where(iota((1, width), 1) >= width // 2, 0.25, 0.0)
    return jnp.concatenate([both_halves, turn, jnp.zeros((width - 4, width), F32)], axis=0).T


def head_rows(w):
    w = w.astype(F32)
    return jnp.concatenate([w, jnp.zeros((12, w.shape[1]), F32)], axis=0)


def sigmoid(v):
    return 0.5 * jnp.tanh(0.5 * v) + 0.5


def layer(x, w_half, b_half):
    v = jnp.dot(x, w_half, preferred_element_type=F32) + b_half
    t = jnp.tanh(v)
    q = v * t
    return (v + q).astype(BF16), ((1.0 + t) * ((1.0 + v) - q)).astype(BF16)


def both(row):
    return row + pltpu.roll(row, CH, 1)


def segment_terms(head_t, count, step):
    upper_half = iota((1, 128), 1) >= CH
    half = (iota((1, 128), 1) // CH).astype(F32)
    total = jnp.zeros((1, 128), F32)
    terms = []
    for p in range(8):
        blk = head_t[:, p * 128 : (p + 1) * 128]
        spacing = jnp.where(2.0 * p + half < count, step, 0.0)
        top = blk[:1, :]
        density = jnp.maximum(top, 0.0) + jnp.log1p(jnp.exp(-jnp.abs(top)))
        optical = density * spacing
        other = pltpu.roll(optical, CH, 1)
        before = total + jnp.where(upper_half, other, 0.0)
        total = total + optical + other
        reach = jnp.exp(-before)
        keep = jnp.exp(-optical)
        terms.append((spacing, reach, keep, reach * (1.0 - keep), sigmoid(blk)))
    return terms, jnp.exp(-total)


def forward_kernel(
    geo, fourier, w_in, b_in, w_mid, b_mid, w_head, res_out, rows_out, heads_out, chunks_out, kept_out,
    seg_rows, w_in_half, w_mid_half, heads, kept, sem,
):
    fcol = columns_of(fourier[...])
    geo0, geo1 = geo[:, 0, :], geo[:, 1, :]
    enc, hid = w_in.shape[1:]
    subs = w_in.shape[0]
    turned = (geo0.T, geo1.T)
    maps, ends = [], []
    total = jnp.int32(0)
    for s in range(subs):
        num, first = region_plan(geo0, s)
        amount = (jnp.sum(num).astype(jnp.int32) + CH - 1) // CH
        chunks_out[s] = amount
        w_in_half[s] = w_in[s] * 0.5
        w_mid_half[s] = w_mid[s] * 0.5
        heads[s] = head_rows(w_head[s]).astype(BF16)
        total = total + amount
        ends.append(total)
        src, place = region_map(num, first)
        maps.append((src, place))
        rows_out[s] = region_take(turned, src, place, s)
    seg_rows[...] = jnp.zeros_like(seg_rows)
    per = rows_out.shape[2] // 128

    def copy(slot, at):
        return pltpu.make_async_copy(kept.at[slot], kept_out.at[at], sem.at[slot])

    def step_of(n, carry):
        s, i = find(n, ends)
        slot = n % 2

        @pl.when(n >= 2)
        def _():
            copy(slot, 0).wait()

        lanes = pl.ds(pl.multiple_of(i * 128, 128), 128)
        rows = rows_out[s, :, lanes]
        rows = [rows[w : w + 1, :] for w in range(8)]
        feats = encode(rows[:4], rows[4:], fcol)
        w1, w2 = w_in_half[s], w_mid_half[s]
        b1, b2 = b_in[pl.ds(s, 1), :] * 0.5, b_mid[pl.ds(s, 1), :] * 0.5
        h2_blocks = []
        for q in range(0, CH * SEG, BLOCK):
            feat = jnp.concatenate(feats[q // 128 : (q + BLOCK) // 128], axis=0)
            h1b, slope1 = layer(feat, w1, b1)
            h2b, slope2 = layer(h1b, w2, b2)
            at = 0
            for part in (feat, h1b, h2b, slope1, slope2):
                kept[slot, q : q + BLOCK, at : at + part.shape[1]] = part
                at += part.shape[1]
            h2_blocks.append(h2b)
        h2b = jnp.concatenate(h2_blocks, axis=0)
        copy(slot, s * per + i).start()
        head_t = lax.dot_general(heads[s], h2b, NT, preferred_element_type=F32)[:8]
        heads_out[s * per + i] = head_t
        terms, passed = segment_terms(head_t, rows[3], rows[7])
        colour = jnp.zeros((8, 128), F32)
        for _, _, _, share, tint in terms:
            colour = colour + share * tint
        colour = both(colour)
        seg_rows[s, :, lanes] = jnp.where(iota((8, 128), 0) == 0, passed, colour)
        return carry

    lax.fori_loop(0, total, step_of, 0)

    @pl.when(total >= 1)
    def _():
        copy((total - 1) % 2, 0).wait()

    @pl.when(total >= 2)
    def _():
        copy(total % 2, 0).wait()

    found = []
    for s in range(subs):
        src, place = maps[s]
        wide = src.shape[1]
        mask = (iota((8, wide), 0) == place) & (iota((8, wide), 1) % 128 < CH)
        own = jnp.concatenate(
            [jnp.where(mask, seg_rows[s, r : r + 1, :], 0.0) for r in (1, 2, 3, 0)], axis=0
        )
        full = lax.dot_general(jnp.concatenate(split3(own), axis=0), src, NT, preferred_element_type=F32)
        found.append((full[0:32] + full[32:64]) + full[64:96])
    res_out[...] = jnp.concatenate(
        [found[s][w * 8 : w * 8 + 8, :] for w in range(4) for s in range(subs)], axis=0
    ).T


def merge_kernel(slot, order, target, res, rendered_out, cot_out):
    groups = res.shape[0]
    sl = slot[...]
    entries = sl.shape[1]
    dest = (iota((groups, entries), 0) == sl // 32).astype(F32).astype(BF16)
    full = pick(res[...], dest, TN, True)
    lane = iota((32, entries), 0) == sl % 32
    vals = [
        jnp.sum(jnp.where(lane, full[w * 32 : (w + 1) * 32, :], 0.0), axis=0, keepdims=True)
        for w in range(4)
    ]
    rays = entries // 4
    seg = [[vals[w][:, k * rays : (k + 1) * rays] for w in range(4)] for k in range(4)]
    which = [order[j : j + 1, :] for j in range(4)]
    ordered = []
    for j in range(4):
        ordered.append(
            [sum(jnp.where(which[j] == k, seg[k][w], 0.0) for k in range(4)) for w in range(4)]
        )
    carried = [jnp.ones((1, rays), F32)]
    colour = [jnp.zeros((1, rays), F32)] * 3
    for j in range(4):
        colour = [colour[c] + carried[j] * ordered[j][c] for c in range(3)]
        carried.append(carried[j] * ordered[j][3])
    for c in range(3):
        rendered_out[c : c + 1, :] = colour[c]
    grad = [(colour[c] - target[c : c + 1, :]) * (1.0 / 16.0) for c in range(3)]
    cots = [None] * 4
    tail = jnp.zeros((1, rays), F32)
    for j in (3, 2, 1, 0):
        cots[j] = [carried[j] * g for g in grad] + [carried[j] * tail]
        tail = sum(ordered[j][c] * grad[c] for c in range(3)) + ordered[j][3] * tail
    rows = []
    for w in range(4):
        rows.append(
            jnp.concatenate(
                [sum(jnp.where(which[j] == k, cots[j][w], 0.0) for j in range(4)) for k in range(4)],
                axis=1,
            )
        )
    cot_out[...] = dispatch(sl, rows, groups)


def backward_kernel(
    chunks, geo, cot, rows_in, heads, w_mid, w_head, kept_in, out,
    given, w_mid_half, head_half, g_in, g_mid, g_bin, g_bmid, g_head, kept, sem,
):
    geo0, turned = geo[:, 0, :], cot[...].T
    subs, enc, hid = g_in.shape
    per = rows_in.shape[2] // 128
    ends = []
    total = jnp.int32(0)
    for t in range(subs):
        total = total + chunks[t]
        ends.append(total)

    def copy(slot, at):
        return pltpu.make_async_copy(kept_in.at[at], kept.at[slot], sem.at[slot])

    def fetch(n):
        t, i = find(n, ends)
        copy(n % 2, t * per + i).start()

    @pl.when(total >= 1)
    def _():
        fetch(jnp.int32(0))

    for t in range(subs):
        src, place = region_map(*region_plan(geo0, t))
        rows = region_take((turned,), src, place, t)
        w_mid_half[t] = w_mid[t] * 0.5
        head_half[t] = (head_rows(w_head[t]) * 0.5).astype(BF16)
        given[t] = jnp.concatenate([rows, rows], axis=0)
    for ref in (g_in, g_mid, g_bin, g_bmid, g_head):
        ref[...] = jnp.zeros_like(ref)

    def step_of(n, carry):
        t, i = find(n, ends)
        slot = n % 2

        @pl.when(n + 1 < total)
        def _():
            fetch(n + 1)

        lanes = pl.ds(pl.multiple_of(i * 128, 128), 128)
        rows = rows_in[t, :, lanes]
        cot_rows = given[t, :, lanes]
        terms, passed = segment_terms(heads[t * per + i], rows[3:4, :], rows[7:8, :])
        channel = iota((8, 128), 0)
        paint = jnp.zeros((8, 128), F32)
        for c in range(3):
            paint = jnp.where(channel == c + 1, cot_rows[c : c + 1, :], paint)
        lower_half = iota((1, 128), 1) < CH
        after = cot_rows[3:4, :] * passed
        top_row = channel == 0
        cots = [None] * 8
        for p in range(7, -1, -1):
            spacing, reach, keep, share, tint = terms[p]
            weight = jnp.sum(paint * tint, axis=0, keepdims=True)
            gain = share * weight
            other = pltpu.roll(gain, CH, 1)
            later = after + jnp.where(lower_half, other, 0.0)
            after = after + gain + other
            g_opt = (reach * keep * weight - later) * spacing
            cots[p] = jnp.where(top_row, g_opt * tint, paint * share * tint * (1.0 - tint))
        cot_t = jnp.concatenate(cots, axis=1)
        cot_b = jnp.concatenate([cot_t, jnp.zeros_like(cot_t)], axis=0).astype(BF16)
        copy(slot, 0).wait()
        feat = kept[slot, :, 0:enc]
        h1b = kept[slot, :, enc : enc + hid]
        h2b = kept[slot, :, enc + hid : enc + 2 * hid]
        g_head[t] += jnp.dot(cot_b, h2b, preferred_element_type=F32)
        cot_rows_b = cot_b.astype(F32).T.astype(BF16)
        gz2_blocks, gz1_blocks = [], []
        sum1 = sum2 = jnp.zeros((8, hid), F32)
        for q in range(0, CH * SEG, BLOCKB):
            slope2 = kept[slot, q : q + BLOCKB, enc + 3 * hid : enc + 4 * hid].astype(F32)
            gz2 = jnp.dot(cot_rows_b[q : q + BLOCKB], head_half[t], preferred_element_type=F32) * slope2
            gz2b = gz2.astype(BF16)
            sum2 = sum2 + jnp.sum(gz2.reshape(-1, 8, hid), axis=0)
            slope1 = kept[slot, q : q + BLOCKB, enc + 2 * hid : enc + 3 * hid].astype(F32)
            gz1 = lax.dot_general(gz2b, w_mid_half[t], NT, preferred_element_type=F32) * slope1
            sum1 = sum1 + jnp.sum(gz1.reshape(-1, 8, hid), axis=0)
            gz2_blocks.append(gz2b)
            gz1_blocks.append(gz1.astype(BF16))
        gz2b, gz1b = jnp.concatenate(gz2_blocks, axis=0), jnp.concatenate(gz1_blocks, axis=0)
        g_mid[t] += lax.dot_general(h1b, gz2b, TN, preferred_element_type=F32)
        g_bmid[t] += sum2
        g_bin[t] += sum1
        g_in[t] += lax.dot_general(feat, gz1b, TN, preferred_element_type=F32)
        return carry

    lax.fori_loop(0, total, step_of, 0)
    row = iota((16, hid), 0)
    for t in range(subs):
        out[t, 0:enc, :] = g_in[t].astype(BF16)
        out[t, enc : enc + hid, :] = g_mid[t].astype(BF16)
        b1 = jnp.sum(g_bin[t], axis=0, keepdims=True)
        b2 = jnp.sum(g_bmid[t], axis=0, keepdims=True)
        tail = jnp.where(row == 8, b1, jnp.where(row == 9, b2, g_head[t]))
        out[t, enc + hid : enc + hid + 16, :] = tail.astype(BF16)
        out[t, enc + hid + 16 :, :] = jnp.zeros((PAD - 16, hid), BF16)


def total_kernel(parts, out):
    acc = parts[0].astype(F32)
    for i in range(1, parts.shape[0]):
        acc = acc + parts[i].astype(F32)
    out[...] = acc.astype(BF16)


def spread_kernel(packed, o_in, o_bin, o_mid, o_bmid, o_head):
    regions, enc, hid = o_in.shape
    for s in range(regions):
        o_in[s] = packed[s, 0:enc, :].astype(F32)
        o_mid[s] = packed[s, enc : enc + hid, :].astype(F32)
        tail = packed[s, enc + hid : enc + hid + 16, :].astype(F32)
        o_head[s] = tail[0:4, :]
        o_bin[s : s + 1, :] = tail[8:9, :]
        o_bmid[s : s + 1, :] = tail[9:10, :]


def call(kernel, outs, *args, **more):
    return pl.pallas_call(
        kernel,
        out_shape=outs,
        compiler_params=pltpu.CompilerParams(vmem_limit_bytes=56 * 2**20),
        **more,
    )(*args)


def struct(*shape, dtype=F32):
    return jax.ShapeDtypeStruct(shape, dtype)


def a2a(x, axis):
    return lax.all_to_all(x, axis, split_axis=0, concat_axis=0, tiled=True)


def body(
    anchor, direction, seg_start, seg_step, counts, routes, order, target,
    fourier, w_input, b_input, w_middle, b_middle, w_output,
):
    groups = lax.axis_size("region")
    reps = lax.axis_size("rep")
    subs, enc, hid = w_input.shape
    rays = anchor.shape[1]
    geo_send, slot = call(
        send_kernel,
        (struct(groups, 2, 128), struct(1, rays * 4, dtype=jnp.int32)),
        anchor, direction, seg_start, seg_step, counts, routes.T,
    )
    geo = a2a(geo_send, "region")

    wide = groups * 16
    chunk_cap = subs * groups * 8 // CH
    width = enc + 4 * hid
    any_spec, vm_spec = pl.BlockSpec(memory_space=pl.ANY), pl.BlockSpec(memory_space=pltpu.VMEM)
    sm_spec = pl.BlockSpec(memory_space=pltpu.SMEM)
    res, seg_geo, heads, chunks, kept = call(
        forward_kernel,
        (
            struct(groups, 128), struct(subs, 8, wide), struct(chunk_cap, 8, CH * SEG),
            struct(subs, dtype=jnp.int32), struct(chunk_cap, CH * SEG, width, dtype=BF16),
        ),
        geo, fourier, w_input, b_input, w_middle, b_middle, w_output,
        out_specs=(vm_spec, vm_spec, vm_spec, sm_spec, any_spec),
        scratch_shapes=[
            VM((subs, 8, wide), F32), VM((subs, enc, hid), BF16), VM((subs, hid, hid), BF16), VM((subs, 16, hid), BF16),
            VM((2, CH * SEG, width), BF16), pltpu.SemaphoreType.DMA((2,)),
        ],
    )
    res_back = a2a(res[:, None, :], "region")[:, 0, :]
    rendered, cot_send = call(
        merge_kernel,
        (struct(3, rays), struct(groups, 128)),
        slot, order.T, target, res_back,
    )
    cot = a2a(cot_send[:, None, :], "region")[:, 0, :]
    rows = enc + hid + PAD
    packed = call(
        backward_kernel,
        struct(subs, rows, hid, dtype=BF16),
        chunks, geo, cot, seg_geo, heads, w_middle, w_output, kept,
        in_specs=[sm_spec] + [vm_spec] * 6 + [any_spec],
        scratch_shapes=[
            VM((subs, 8, wide), F32), VM((subs, hid, hid), BF16), VM((subs, 16, hid), BF16),
            VM((subs, enc, hid), F32), VM((subs, hid, hid), F32), VM((subs, 8, hid), F32), VM((subs, 8, hid), F32),
            VM((subs, 16, hid), F32), VM((2, CH * SEG, width), BF16), pltpu.SemaphoreType.DMA((2,)),
        ],
    )
    parts = a2a(packed.reshape(reps, subs * rows // reps, hid), "rep")
    mine = call(total_kernel, struct(*parts.shape[1:], dtype=BF16), parts)
    pairs = [[r, r + 1] for r in range(0, reps, 2)]
    strides = [list(range(k, reps, 2)) for k in range(2)]
    for members in (pairs, strides):
        mine = lax.all_gather(mine, "rep", axis=0, tiled=True, axis_index_groups=members)
    full = mine.reshape(subs, rows, hid)
    grads = call(
        spread_kernel,
        (struct(subs, enc, hid), struct(subs, hid), struct(subs, hid, hid), struct(subs, hid), struct(subs, 4, hid)),
        full,
    )
    return (rendered, *grads)


def solution(mesh):
    rays, own = ("rep", "region"), "region"
    return jax.shard_map(
        body,
        mesh=mesh,
        in_specs=(
            P(None, rays), P(None, rays), P(None, rays), P(None, rays), P(None, rays),
            P(rays, None), P(rays, None), P(None, rays), P(),
            P(own, None, None), P(own, None), P(own, None, None), P(own, None), P(own, None, None),
        ),
        out_specs=(
            P(None, rays), P(own, None, None), P(own, None), P(own, None, None), P(own, None), P(own, None, None),
        ),
        check_vma=False,
    )
```

```python
import functools
import math

import jax
import jax.numpy as jnp
import numpy as np
from jax import lax
from jax.experimental import pallas as pl
from jax.experimental.pallas import tpu as pltpu
from jax.sharding import PartitionSpec as P

SEG = 16
BLOCK = 256
BLOCKB = 512
PAD = 32
CH = 64
F32, BF16 = jnp.float32, jnp.bfloat16
VM = pltpu.VMEM
NT = (((1,), (1,)), ((), ()))
TN = (((0,), (0,)), ((), ()))


def _sine_coeffs():
    k = np.arange(64)
    y = 0.125 + 0.125 * np.cos(math.pi * (k + 0.5) / 64)
    r = np.sqrt(y)
    poly = np.polynomial.chebyshev.Chebyshev.interpolate(
        lambda q: np.sin(2 * math.pi * np.sqrt(q)) / np.sqrt(q), 5, domain=[1e-12, 0.25]
    )
    return [float(c) for c in poly.convert(kind=np.polynomial.Polynomial).coef]


COEF = _sine_coeffs()


def sine_turns(u):
    r = u - jnp.round(u)
    y = r * r
    p = jnp.full_like(y, COEF[5])
    for c in COEF[4::-1]:
        p = p * y + c
    return p * r


def split3(x):
    hi = x.astype(BF16)
    rest = x - hi.astype(F32)
    mid = rest.astype(BF16)
    low = (rest - mid.astype(F32)).astype(BF16)
    return hi, mid, low


def pick(a, b, dims, split_first):
    if split_first:
        parts = [lax.dot_general(x, b, dims, preferred_element_type=F32) for x in split3(a)]
    else:
        parts = [lax.dot_general(a, x, dims, preferred_element_type=F32) for x in split3(b)]
    return (parts[0] + parts[1]) + parts[2]


def iota(shape, dim):
    return lax.broadcasted_iota(jnp.int32, shape, dim)


def dispatch(slot, vals, groups):
    entries = slot.shape[1]
    dest = (iota((groups, entries), 0) == slot // 32).astype(F32).astype(BF16)
    lane = iota((32, entries), 0) == slot % 32
    rows = jnp.concatenate([jnp.where(lane, v, 0.0) for v in vals], axis=0)
    return pick(dest, rows, NT, False)


def send_kernel(anchor, direction, start, step, counts, routes, geo_out, slot_out):
    groups = geo_out.shape[0]
    regs = jnp.concatenate([routes[k : k + 1, :] for k in range(4)], axis=1)
    entries = regs.shape[1]
    regions = groups * 4
    hot = (iota((regions, entries), 0) == regs).astype(F32)
    upper = (iota((entries, entries), 0) < iota((entries, entries), 1)).astype(F32).astype(BF16)
    earlier = jnp.dot(hot.astype(BF16), upper, preferred_element_type=F32)
    rank = jnp.sum(hot * earlier, axis=0, keepdims=True).astype(jnp.int32)
    slot = regs * 8 + rank
    slot_out[...] = slot
    stp = step[...].astype(F32)
    cnt = counts[...].astype(F32)
    rows = []
    for c in range(3):
        rows.append(
            jnp.concatenate(
                [anchor[c : c + 1, :] + start[k : k + 1, :] * direction[c : c + 1, :] for k in range(4)],
                axis=1,
            )
        )
    rows.append(jnp.concatenate([cnt[k : k + 1, :] for k in range(4)], axis=1))
    for c in range(3):
        rows.append(
            jnp.concatenate([stp[k : k + 1, :] * direction[c : c + 1, :] for k in range(4)], axis=1)
        )
    rows.append(jnp.concatenate([stp[k : k + 1, :] for k in range(4)], axis=1))
    geo_out[:, 0, :] = dispatch(slot, rows[:4], groups)
    geo_out[:, 1, :] = dispatch(slot, rows[4:], groups)


def region_plan(geo0, s):
    groups = geo0.shape[0]
    lanes = iota((groups, 128), 1)
    live = jnp.where((lanes // 8 == 12 + s) & (geo0 > 0.5), 1.0, 0.0)
    num = jnp.sum(live, axis=1, keepdims=True)
    before = iota((groups, groups), 1) < iota((groups, groups), 0)
    first = jnp.dot(
        before.astype(F32).astype(BF16),
        jnp.broadcast_to(num, (groups, 128)).astype(BF16),
        preferred_element_type=F32,
    )[:, :1]
    return num, first


def region_map(num, first):
    groups = num.shape[0]
    wide = groups * 8 * 2
    lane = iota((groups, wide), 1)
    j = (lane // 128 * CH + lane % CH).astype(F32)
    src = jnp.where((j >= first) & (j < first + num), 1.0, 0.0)
    place = (j[:1, :] - jnp.sum(src * first, axis=0, keepdims=True)).astype(jnp.int32)
    return src.astype(BF16), place


def region_take(arrs, src, place, s):
    own = jnp.concatenate([a[w * 32 + s * 8 : w * 32 + s * 8 + 8, :] for a in arrs for w in range(4)], axis=0)
    found = jnp.dot(jnp.concatenate(split3(own), axis=0), src, preferred_element_type=F32)
    rows = own.shape[0]
    full = (found[:rows] + found[rows : 2 * rows]) + found[2 * rows :]
    mask = iota((8, src.shape[1]), 0) == place
    return jnp.concatenate(
        [
            jnp.sum(jnp.where(mask, full[r : r + 8, :], 0.0), axis=0, keepdims=True)
            for r in range(0, rows, 8)
        ],
        axis=0,
    )


def find(n, ends):
    s = sum((n >= e).astype(jnp.int32) for e in ends[:-1])
    start = jnp.int32(0)
    for e in ends[:-1]:
        start = jnp.where(n >= e, e, start)
    return s, n - start


def encode(head, rest, fcol):
    px, py, pz, count = head
    dx, dy, dz, step = rest
    fx, fy, fz, turn = (fcol[:, c : c + 1] for c in range(4))
    begin = px * fx + py * fy + pz * fz
    slope = dx * fx + dy * fy + dz * fz
    half = (iota((1, 128), 1) // CH).astype(F32)
    begin = begin + (half + 0.5) * slope + turn
    begin = (begin - jnp.round(begin)).T
    slope = (slope - jnp.round(slope)).T
    slope = slope + slope
    feats = []
    for p in range(8):
        feats.append(sine_turns(begin).astype(BF16))
        begin = begin + slope
    return feats


def columns_of(fourier):
    both_halves = jnp.concatenate([fourier, fourier], axis=1)
    width = both_halves.shape[1]
    turn = jnp.where(iota((1, width), 1) >= width // 2, 0.25, 0.0)
    return jnp.concatenate([both_halves, turn, jnp.zeros((width - 4, width), F32)], axis=0).T


def head_rows(w):
    w = w.astype(F32)
    return jnp.concatenate([w, jnp.zeros((12, w.shape[1]), F32)], axis=0)


def sigmoid(v):
    return 0.5 * jnp.tanh(0.5 * v) + 0.5


def layer(x, w_half, b_half):
    v = jnp.dot(x, w_half, preferred_element_type=F32) + b_half
    t = jnp.tanh(v)
    q = v * t
    return (v + q).astype(BF16), ((1.0 + t) * ((1.0 + v) - q)).astype(BF16)


def both(row):
    return row + pltpu.roll(row, CH, 1)


def segment_terms(head_t, count, step):
    upper_half = iota((1, 128), 1) >= CH
    half = (iota((1, 128), 1) // CH).astype(F32)
    total = jnp.zeros((1, 128), F32)
    terms = []
    for p in range(8):
        blk = head_t[:, p * 128 : (p + 1) * 128]
        spacing = jnp.where(2.0 * p + half < count, step, 0.0)
        top = blk[:1, :]
        density = jnp.maximum(top, 0.0) + jnp.log1p(jnp.exp(-jnp.abs(top)))
        optical = density * spacing
        other = pltpu.roll(optical, CH, 1)
        before = total + jnp.where(upper_half, other, 0.0)
        total = total + optical + other
        reach = jnp.exp(-before)
        keep = jnp.exp(-optical)
        terms.append((spacing, reach, keep, reach * (1.0 - keep), sigmoid(blk)))
    return terms, jnp.exp(-total)


def forward_kernel(
    geo, fourier, w_in, b_in, w_mid, b_mid, w_head, res_out, rows_out, heads_out, chunks_out, src_out, place_out, kept_out,
    seg_rows, w_in_half, w_mid_half, heads, kept, sem,
):
    fcol = columns_of(fourier[...])
    geo0, geo1 = geo[:, 0, :], geo[:, 1, :]
    enc, hid = w_in.shape[1:]
    subs = w_in.shape[0]
    turned = (geo0.T, geo1.T)
    maps, ends = [], []
    total = jnp.int32(0)
    for s in range(subs):
        num, first = region_plan(geo0, s)
        amount = (jnp.sum(num).astype(jnp.int32) + CH - 1) // CH
        chunks_out[s] = amount
        w_in_half[s] = w_in[s] * 0.5
        w_mid_half[s] = w_mid[s] * 0.5
        heads[s] = head_rows(w_head[s]).astype(BF16)
        total = total + amount
        ends.append(total)
        src, place = region_map(num, first)
        maps.append((src, place))
        src_out[s] = src
        place_out[s] = place
        rows_out[s] = region_take(turned, src, place, s)
    seg_rows[...] = jnp.zeros_like(seg_rows)
    per = rows_out.shape[2] // 128

    def copy(slot, at):
        return pltpu.make_async_copy(kept.at[slot], kept_out.at[at], sem.at[slot])

    def step_of(n, carry):
        s, i = find(n, ends)
        slot = n % 2

        @pl.when(n >= 2)
        def _():
            copy(slot, 0).wait()

        lanes = pl.ds(pl.multiple_of(i * 128, 128), 128)
        rows = rows_out[s, :, lanes]
        rows = [rows[w : w + 1, :] for w in range(8)]
        feats = encode(rows[:4], rows[4:], fcol)
        w1, w2 = w_in_half[s], w_mid_half[s]
        b1, b2 = b_in[pl.ds(s, 1), :] * 0.5, b_mid[pl.ds(s, 1), :] * 0.5
        h2_blocks = []
        for q in range(0, CH * SEG, BLOCK):
            feat = jnp.concatenate(feats[q // 128 : (q + BLOCK) // 128], axis=0)
            h1b, slope1 = layer(feat, w1, b1)
            h2b, slope2 = layer(h1b, w2, b2)
            at = 0
            for part in (feat, h1b, h2b, slope1, slope2):
                kept[slot, q : q + BLOCK, at : at + part.shape[1]] = part
                at += part.shape[1]
            h2_blocks.append(h2b)
        h2b = jnp.concatenate(h2_blocks, axis=0)
        copy(slot, s * per + i).start()
        head_t = lax.dot_general(heads[s], h2b, NT, preferred_element_type=F32)[:8]
        heads_out[s * per + i] = head_t
        terms, passed = segment_terms(head_t, rows[3], rows[7])
        colour = jnp.zeros((8, 128), F32)
        for _, _, _, share, tint in terms:
            colour = colour + share * tint
        colour = both(colour)
        seg_rows[s, :, lanes] = jnp.where(iota((8, 128), 0) == 0, passed, colour)
        return carry

    lax.fori_loop(0, total, step_of, 0)

    @pl.when(total >= 1)
    def _():
        copy((total - 1) % 2, 0).wait()

    @pl.when(total >= 2)
    def _():
        copy(total % 2, 0).wait()

    found = []
    for s in range(subs):
        src, place = maps[s]
        wide = src.shape[1]
        mask = (iota((8, wide), 0) == place) & (iota((8, wide), 1) % 128 < CH)
        own = jnp.concatenate(
            [jnp.where(mask, seg_rows[s, r : r + 1, :], 0.0) for r in (1, 2, 3, 0)], axis=0
        )
        full = lax.dot_general(jnp.concatenate(split3(own), axis=0), src, NT, preferred_element_type=F32)
        found.append((full[0:32] + full[32:64]) + full[64:96])
    res_out[...] = jnp.concatenate(
        [found[s][w * 8 : w * 8 + 8, :] for w in range(4) for s in range(subs)], axis=0
    ).T


def merge_kernel(slot, order, target, res, rendered_out, cot_out):
    groups = res.shape[0]
    sl = slot[...]
    entries = sl.shape[1]
    dest = (iota((groups, entries), 0) == sl // 32).astype(F32).astype(BF16)
    full = pick(res[...], dest, TN, True)
    lane = iota((32, entries), 0) == sl % 32
    vals = [
        jnp.sum(jnp.where(lane, full[w * 32 : (w + 1) * 32, :], 0.0), axis=0, keepdims=True)
        for w in range(4)
    ]
    rays = entries // 4
    seg = [[vals[w][:, k * rays : (k + 1) * rays] for w in range(4)] for k in range(4)]
    which = [order[j : j + 1, :] for j in range(4)]
    ordered = []
    for j in range(4):
        ordered.append(
            [sum(jnp.where(which[j] == k, seg[k][w], 0.0) for k in range(4)) for w in range(4)]
        )
    carried = [jnp.ones((1, rays), F32)]
    colour = [jnp.zeros((1, rays), F32)] * 3
    for j in range(4):
        colour = [colour[c] + carried[j] * ordered[j][c] for c in range(3)]
        carried.append(carried[j] * ordered[j][3])
    for c in range(3):
        rendered_out[c : c + 1, :] = colour[c]
    grad = [(colour[c] - target[c : c + 1, :]) * (1.0 / 16.0) for c in range(3)]
    cots = [None] * 4
    tail = jnp.zeros((1, rays), F32)
    for j in (3, 2, 1, 0):
        cots[j] = [carried[j] * g for g in grad] + [carried[j] * tail]
        tail = sum(ordered[j][c] * grad[c] for c in range(3)) + ordered[j][3] * tail
    rows = []
    for w in range(4):
        rows.append(
            jnp.concatenate(
                [sum(jnp.where(which[j] == k, cots[j][w], 0.0) for j in range(4)) for k in range(4)],
                axis=1,
            )
        )
    cot_out[...] = dispatch(sl, rows, groups)


def backward_kernel(
    chunks, src_in, place_in, cot, rows_in, heads, w_mid, w_head, kept_in, out,
    given, w_mid_half, head_half, g_in, g_mid, g_bin, g_bmid, g_head, kept, sem,
):
    turned = cot[...].T
    subs, enc, hid = g_in.shape
    per = rows_in.shape[2] // 128
    ends = []
    total = jnp.int32(0)
    for t in range(subs):
        total = total + chunks[t]
        ends.append(total)

    def copy(slot, at):
        return pltpu.make_async_copy(kept_in.at[at], kept.at[slot], sem.at[slot])

    def fetch(n):
        t, i = find(n, ends)
        copy(n % 2, t * per + i).start()

    @pl.when(total >= 1)
    def _():
        fetch(jnp.int32(0))

    for t in range(subs):
        rows = region_take((turned,), src_in[t], place_in[t], t)
        w_mid_half[t] = w_mid[t] * 0.5
        head_half[t] = (head_rows(w_head[t]) * 0.5).astype(BF16)
        given[t] = jnp.concatenate([rows, rows], axis=0)
    for ref in (g_in, g_mid, g_bin, g_bmid, g_head):
        ref[...] = jnp.zeros_like(ref)

    def step_of(n, carry):
        t, i = find(n, ends)
        slot = n % 2

        @pl.when(n + 1 < total)
        def _():
            fetch(n + 1)

        lanes = pl.ds(pl.multiple_of(i * 128, 128), 128)
        rows = rows_in[t, :, lanes]
        cot_rows = given[t, :, lanes]
        terms, passed = segment_terms(heads[t * per + i], rows[3:4, :], rows[7:8, :])
        channel = iota((8, 128), 0)
        paint = jnp.zeros((8, 128), F32)
        for c in range(3):
            paint = jnp.where(channel == c + 1, cot_rows[c : c + 1, :], paint)
        lower_half = iota((1, 128), 1) < CH
        after = cot_rows[3:4, :] * passed
        top_row = channel == 0
        cots = [None] * 8
        for p in range(7, -1, -1):
            spacing, reach, keep, share, tint = terms[p]
            weight = jnp.sum(paint * tint, axis=0, keepdims=True)
            gain = share * weight
            other = pltpu.roll(gain, CH, 1)
            later = after + jnp.where(lower_half, other, 0.0)
            after = after + gain + other
            g_opt = (reach * keep * weight - later) * spacing
            cots[p] = jnp.where(top_row, g_opt * tint, paint * share * tint * (1.0 - tint))
        cot_t = jnp.concatenate(cots, axis=1)
        cot_b = jnp.concatenate([cot_t, jnp.zeros_like(cot_t)], axis=0).astype(BF16)
        copy(slot, 0).wait()
        feat = kept[slot, :, 0:enc]
        h1b = kept[slot, :, enc : enc + hid]
        h2b = kept[slot, :, enc + hid : enc + 2 * hid]
        g_head[t] += jnp.dot(cot_b, h2b, preferred_element_type=F32)
        cot_rows_b = cot_b.astype(F32).T.astype(BF16)
        gz2_blocks, gz1_blocks = [], []
        sum1 = sum2 = jnp.zeros((8, hid), F32)
        for q in range(0, CH * SEG, BLOCKB):
            slope2 = kept[slot, q : q + BLOCKB, enc + 3 * hid : enc + 4 * hid].astype(F32)
            gz2 = jnp.dot(cot_rows_b[q : q + BLOCKB], head_half[t], preferred_element_type=F32) * slope2
            gz2b = gz2.astype(BF16)
            sum2 = sum2 + jnp.sum(gz2.reshape(-1, 8, hid), axis=0)
            slope1 = kept[slot, q : q + BLOCKB, enc + 2 * hid : enc + 3 * hid].astype(F32)
            gz1 = lax.dot_general(gz2b, w_mid_half[t], NT, preferred_element_type=F32) * slope1
            sum1 = sum1 + jnp.sum(gz1.reshape(-1, 8, hid), axis=0)
            gz2_blocks.append(gz2b)
            gz1_blocks.append(gz1.astype(BF16))
        gz2b, gz1b = jnp.concatenate(gz2_blocks, axis=0), jnp.concatenate(gz1_blocks, axis=0)
        g_mid[t] += lax.dot_general(h1b, gz2b, TN, preferred_element_type=F32)
        g_bmid[t] += sum2
        g_bin[t] += sum1
        g_in[t] += lax.dot_general(feat, gz1b, TN, preferred_element_type=F32)
        return carry

    lax.fori_loop(0, total, step_of, 0)
    row = iota((16, hid), 0)
    for t in range(subs):
        out[t, 0:enc, :] = g_in[t].astype(BF16)
        out[t, enc : enc + hid, :] = g_mid[t].astype(BF16)
        b1 = jnp.sum(g_bin[t], axis=0, keepdims=True)
        b2 = jnp.sum(g_bmid[t], axis=0, keepdims=True)
        tail = jnp.where(row == 8, b1, jnp.where(row == 9, b2, g_head[t]))
        out[t, enc + hid : enc + hid + 16, :] = tail.astype(BF16)
        out[t, enc + hid + 16 :, :] = jnp.zeros((PAD - 16, hid), BF16)


def total_kernel(parts, out):
    acc = parts[0].astype(F32)
    for i in range(1, parts.shape[0]):
        acc = acc + parts[i].astype(F32)
    out[...] = acc.astype(BF16)


def spread_kernel(packed, o_in, o_bin, o_mid, o_bmid, o_head):
    regions, enc, hid = o_in.shape
    for s in range(regions):
        o_in[s] = packed[s, 0:enc, :].astype(F32)
        o_mid[s] = packed[s, enc : enc + hid, :].astype(F32)
        tail = packed[s, enc + hid : enc + hid + 16, :].astype(F32)
        o_head[s] = tail[0:4, :]
        o_bin[s : s + 1, :] = tail[8:9, :]
        o_bmid[s : s + 1, :] = tail[9:10, :]


def call(kernel, outs, *args, **more):
    return pl.pallas_call(
        kernel,
        out_shape=outs,
        compiler_params=pltpu.CompilerParams(vmem_limit_bytes=56 * 2**20),
        **more,
    )(*args)


def struct(*shape, dtype=F32):
    return jax.ShapeDtypeStruct(shape, dtype)


def a2a(x, axis):
    return lax.all_to_all(x, axis, split_axis=0, concat_axis=0, tiled=True)


def body(
    anchor, direction, seg_start, seg_step, counts, routes, order, target,
    fourier, w_input, b_input, w_middle, b_middle, w_output,
):
    groups = lax.axis_size("region")
    reps = lax.axis_size("rep")
    subs, enc, hid = w_input.shape
    rays = anchor.shape[1]
    geo_send, slot = call(
        send_kernel,
        (struct(groups, 2, 128), struct(1, rays * 4, dtype=jnp.int32)),
        anchor, direction, seg_start, seg_step, counts, routes.T,
    )
    geo = a2a(geo_send, "region")

    wide = groups * 16
    chunk_cap = subs * groups * 8 // CH
    width = enc + 4 * hid
    any_spec, vm_spec = pl.BlockSpec(memory_space=pl.ANY), pl.BlockSpec(memory_space=pltpu.VMEM)
    sm_spec = pl.BlockSpec(memory_space=pltpu.SMEM)
    res, seg_geo, heads, chunks, src, place, kept = call(
        forward_kernel,
        (
            struct(groups, 128), struct(subs, 8, wide), struct(chunk_cap, 8, CH * SEG),
            struct(subs, dtype=jnp.int32), struct(subs, groups, wide, dtype=BF16),
            struct(subs, 1, wide, dtype=jnp.int32), struct(chunk_cap, CH * SEG, width, dtype=BF16),
        ),
        geo, fourier, w_input, b_input, w_middle, b_middle, w_output,
        out_specs=(vm_spec, vm_spec, vm_spec, sm_spec, vm_spec, vm_spec, any_spec),
        scratch_shapes=[
            VM((subs, 8, wide), F32), VM((subs, enc, hid), BF16), VM((subs, hid, hid), BF16), VM((subs, 16, hid), BF16),
            VM((2, CH * SEG, width), BF16), pltpu.SemaphoreType.DMA((2,)),
        ],
    )
    res_back = a2a(res[:, None, :], "region")[:, 0, :]
    rendered, cot_send = call(
        merge_kernel,
        (struct(3, rays), struct(groups, 128)),
        slot, order.T, target, res_back,
    )
    cot = a2a(cot_send[:, None, :], "region")[:, 0, :]
    rows = enc + hid + PAD
    packed = call(
        backward_kernel,
        struct(subs, rows, hid, dtype=BF16),
        chunks, src, place, cot, seg_geo, heads, w_middle, w_output, kept,
        in_specs=[sm_spec] + [vm_spec] * 7 + [any_spec],
        scratch_shapes=[
            VM((subs, 8, wide), F32), VM((subs, hid, hid), BF16), VM((subs, 16, hid), BF16),
            VM((subs, enc, hid), F32), VM((subs, hid, hid), F32), VM((subs, 8, hid), F32), VM((subs, 8, hid), F32),
            VM((subs, 16, hid), F32), VM((2, CH * SEG, width), BF16), pltpu.SemaphoreType.DMA((2,)),
        ],
    )
    parts = a2a(packed.reshape(reps, subs * rows // reps, hid), "rep")
    mine = call(total_kernel, struct(*parts.shape[1:], dtype=BF16), parts)
    pairs = [[r, r + 1] for r in range(0, reps, 2)]
    strides = [list(range(k, reps, 2)) for k in range(2)]
    for members in (pairs, strides):
        mine = lax.all_gather(mine, "rep", axis=0, tiled=True, axis_index_groups=members)
    full = mine.reshape(subs, rows, hid)
    grads = call(
        spread_kernel,
        (struct(subs, enc, hid), struct(subs, hid), struct(subs, hid, hid), struct(subs, hid), struct(subs, 4, hid)),
        full,
    )
    return (rendered, *grads)


def solution(mesh):
    rays, own = ("rep", "region"), "region"
    return jax.shard_map(
        body,
        mesh=mesh,
        in_specs=(
            P(None, rays), P(None, rays), P(None, rays), P(None, rays), P(None, rays),
            P(rays, None), P(rays, None), P(None, rays), P(),
            P(own, None, None), P(own, None), P(own, None, None), P(own, None), P(own, None, None),
        ),
        out_specs=(
            P(None, rays), P(own, None, None), P(own, None), P(own, None, None), P(own, None), P(own, None, None),
        ),
        check_vma=False,
    )
```
